256 devices in a mesh: dp: 32 (over z, x), tensor: 8 (over y, core).
Axes of the slice: x: 4, y: 4, z: 8, core: 2. Of those that a mesh axis runs over, the one named last changes fastest.
Arguments:
- normed_input_rows: bfloat16 [16384, 8192], P('dp', 'tensor'), may hold values from -6 to 6
- key_value_cotangent: bfloat16 [16384, 2, 1024], P('dp', None, 'tensor'), may hold values from -24 to 24
- key_value_weight: bfloat16 [2, 8192, 1024], P(None, None, 'tensor'), may hold values from -0.0625 to 0.0625
- adapter_down_factors: bfloat16 [512, 8192], P('dp', 'tensor'), may hold values from -0.0625 to 0.0625
- adapter_up_factors: bfloat16 [512, 1024], P('dp', 'tensor'), may hold values from -0.1875 to 0.1875
- slot_adapter: int32 [8], replicated, may hold values from 0 to 7, each once
- adapter_of_block: int32 [128], P('dp'), may hold values from 0 to 7, as said below
- live_rows_of_block: int32 [128], P('dp'), may hold values from 16 to 128
- prompt_of_block: int32 [128], P('dp'), may hold values from 0 to 15, as said below
- reward_of_block: float32 [128], P('dp'), may hold values from 0 to 4
Outputs:
- input_gradient: bfloat16 [16384, 8192], P('dp', 'tensor')
- grad_a: float32 [512, 8192], P('dp', 'tensor')
- grad_b: float32 [512, 1024], P('dp', 'tensor')
The draws below stay inside these ranges and needn't reach their ends.
Inputs may be any that keep to these rules, and one draw needn't show every extreme that they name: `slot_adapter`: each adapter appears once. `adapter_of_block`: among the blocks of one index of dp an adapter repeats only after all 8 have appeared. `prompt_of_block`: each prompt has exactly 8 blocks.
All inputs are finite; a program needn't handle non-finite values.
Results may differ from the reference program's by a relative error of at most 0.0051.
Values may be sent and summed in bfloat16 or wider, within the bound.
No kernel may reach another device: no remote copies, remote signals or barrier semaphores. Data moves between devices by JAX's collectives and lax.ppermute only.
A program may use at most 128 MiB of HBM per device.

```python
import jax
import jax.numpy as jnp
from jax import lax

MODEL_WIDTH = 8192
PROJECTION_SPAN = 1024
ADAPTER_RANK = 64
BLOCK = 128
GSIZE = 8
BLK_DEV = 4
ADAPTER_COUNT = 8
BLOCKS = 128
TOKEN_ROWS = 16384
GROUPS = 16


def draw_prompt_of_block(key, part):
    key = jax.random.fold_in(key, 7)
    return (jax.random.permutation(key, BLOCKS) // GSIZE).astype(jnp.int32)


def draw_adapter_of_block(key, part):
    key = jax.random.fold_in(key, 11)
    device_keys = jax.random.split(key, BLOCKS // BLK_DEV)
    orders = jax.vmap(lambda k: jax.random.permutation(k, ADAPTER_COUNT))(device_keys)
    places = jnp.arange(BLK_DEV, dtype=jnp.int32) % ADAPTER_COUNT
    return orders[:, places].reshape(BLOCKS).astype(jnp.int32)


def with_ends(entries, stream_key, low, high):
    shape = entries.shape
    index_at = [jax.random.randint(jax.random.fold_in(stream_key, axis), (), 0, shape[axis]) for axis in range(len(shape))]
    entries = entries.at[tuple(index_at)].set(low)
    longest = shape.index(max(shape))
    index_at[longest] = (index_at[longest] + 1) % shape[longest]
    return entries.at[tuple(index_at)].set(high)


def levels(own_key, shape, cuts, low, largest):
    gain, own = 1.0, jax.random.fold_in(own_key, 6)
    for position, parts in cuts:
        heights = jnp.exp(jax.random.uniform(jax.random.fold_in(own, position), (parts,), jnp.float32, low / len(cuts), largest / len(cuts)))
        gain = gain * jnp.repeat(heights, shape[position] // parts).reshape([-1 if axis == position else 1 for axis in range(len(shape))])
    return gain


def centred(own_key, dims, spread, reach, cuts=(), kind=jnp.bfloat16):
    array = jax.random.normal(own_key, dims, jnp.float32) * spread
    if len(cuts) > 0:
        array = levels(own_key, dims, cuts, -0.22, 0.18) * array
    return jnp.clip(array, min=-reach, max=reach).astype(kind)


def setup_inputs(seed: int = 0) -> dict:
    splits = jax.random.split(jax.random.key(seed), 11)
    return {
        "normed_input_rows": centred(splits[0], (TOKEN_ROWS, MODEL_WIDTH), 1.0, 6.0, ((0, 32), (1, 8))),
        "key_value_cotangent": centred(splits[1], (TOKEN_ROWS, 2, PROJECTION_SPAN), 4.0, 24.0, ((0, 32), (2, 8))),
        "key_value_weight": centred(splits[2], (2, MODEL_WIDTH, PROJECTION_SPAN), MODEL_WIDTH ** -0.5, 0.0625, ((2, 8),)),
        "adapter_down_factors": centred(splits[3], (ADAPTER_COUNT * ADAPTER_RANK, MODEL_WIDTH), MODEL_WIDTH ** -0.5, 0.0625, ((0, 32), (1, 8))),
        "adapter_up_factors": centred(splits[4], (ADAPTER_COUNT * ADAPTER_RANK, PROJECTION_SPAN), PROJECTION_SPAN ** -0.5, 0.1875, ((0, 32), (1, 8))),
        "slot_adapter": jax.random.permutation(splits[5], ADAPTER_COUNT).astype(jnp.int32),
        "adapter_of_block": draw_adapter_of_block(jax.random.fold_in(splits[10], 71), 0),
        "live_rows_of_block": with_ends(jax.random.randint(splits[7], (BLOCKS,), BLOCK // 8, BLOCK + 1), jax.random.fold_in(splits[7], 1), BLOCK // 8, BLOCK).astype(jnp.int32),
        "prompt_of_block": draw_prompt_of_block(jax.random.fold_in(splits[10], 71), 0),
        "reward_of_block": jnp.clip(4.0 * jax.random.uniform(splits[9], (BLOCKS,), jnp.float32) ** levels(splits[9], (BLOCKS,), ((0, 32),), -0.2, 0.2), 0.0, 4.0),
    }


lowrank_multiplier = 2.0

def reference(normed_input_rows, key_value_cotangent, key_value_weight, adapter_down_factors, adapter_up_factors, slot_adapter, adapter_of_block, live_rows_of_block, prompt_of_block, reward_of_block):
    member = (prompt_of_block[:, None] == jnp.arange(GROUPS, dtype=jnp.int32)[None, :]).astype(jnp.float32)
    totals = lax.optimization_barrier(jnp.sum(member * reward_of_block[:, None], axis=0))
    squares = lax.optimization_barrier(jnp.sum(member * (reward_of_block * reward_of_block)[:, None], axis=0))
    mean_g = totals / GSIZE
    spread_g = jnp.sqrt(jnp.maximum(squares / GSIZE - mean_g * mean_g, 1.0))
    advantage = (reward_of_block - mean_g[prompt_of_block]) / spread_g[prompt_of_block]
    live_mask = jnp.arange(BLOCK, dtype=jnp.int32)[None, :] < live_rows_of_block[:, None]
    coef = jnp.where(live_mask, -advantage[:, None] / GSIZE, 0.0).astype(jnp.float32)
    weighted = (key_value_cotangent.reshape(BLOCKS, BLOCK, 2, PROJECTION_SPAN).astype(jnp.float32) * coef[:, :, None, None]).astype(jnp.bfloat16)
    inverse = jnp.zeros((ADAPTER_COUNT,), jnp.int32).at[slot_adapter].set(jnp.arange(ADAPTER_COUNT, dtype=jnp.int32))
    slot_of = inverse[adapter_of_block]
    down_factor_table = adapter_down_factors.reshape(ADAPTER_COUNT, ADAPTER_RANK, MODEL_WIDTH)
    up_factor_table = adapter_up_factors.reshape(ADAPTER_COUNT, ADAPTER_RANK, PROJECTION_SPAN)
    segment_shrink_matrix = down_factor_table[slot_of].astype(jnp.float32)
    b_block = up_factor_table[slot_of].astype(jnp.float32)
    block_input_rows = normed_input_rows.reshape(BLOCKS, BLOCK, MODEL_WIDTH).astype(jnp.float32)
    value_cotangent = weighted[:, :, 1, :].astype(jnp.float32)
    rank_hidden = jnp.einsum('xqg,xlg->xql', block_input_rows, segment_shrink_matrix).astype(jnp.bfloat16)
    narrow_derivative = jnp.einsum('bkc,brc->bkr', value_cotangent, b_block).astype(jnp.bfloat16)
    weights_flat = jnp.transpose(key_value_weight, (1, 0, 2)).reshape(MODEL_WIDTH, 2 * PROJECTION_SPAN)
    frozen_term = jnp.dot(weighted.reshape(TOKEN_ROWS, 2 * PROJECTION_SPAN), weights_flat.T, preferred_element_type=jnp.float32)
    correction_summand = lowrank_multiplier * jnp.einsum('dbq,dqz->dbz', narrow_derivative.astype(jnp.float32), segment_shrink_matrix)
    input_gradient = (frozen_term + correction_summand.reshape(TOKEN_ROWS, MODEL_WIDTH)).astype(jnp.bfloat16)
    block_down_gradient = lowrank_multiplier * jnp.einsum('veg,vei->vgi', narrow_derivative.astype(jnp.float32), block_input_rows)
    segment_lift_derivative = lowrank_multiplier * jnp.einsum('sqn,sqx->snx', rank_hidden.astype(jnp.float32), value_cotangent)
    grad_a = jax.ops.segment_sum(block_down_gradient, slot_of, num_segments=ADAPTER_COUNT).reshape(ADAPTER_COUNT * ADAPTER_RANK, MODEL_WIDTH)
    grad_b = jax.ops.segment_sum(segment_lift_derivative, slot_of, num_segments=ADAPTER_COUNT).reshape(ADAPTER_COUNT * ADAPTER_RANK, PROJECTION_SPAN)
    return (input_gradient, grad_a, grad_b)
```

```python
import jax
import jax.numpy as jnp
from jax import lax
from jax.sharding import PartitionSpec as P

BLOCK = 128
GSIZE = 8
GROUPS = 16
SLOTS = 8
RANK = 64
LOWRANK_MULTIPLIER = 2.0
BF = jnp.bfloat16
F32 = jnp.float32


def tensor_pairs(chip_step, core_flip):
    return [
        (y * 2 + c, ((y + chip_step) % 4) * 2 + (c ^ core_flip)) for y in range(4) for c in range(2)
    ]


def dot(a, b, ca, cb):
    return lax.dot_general(a, b, (((ca,), (cb,)), ((), ())), preferred_element_type=F32)


def shards(
    normed_input_rows,
    key_value_cotangent,
    key_value_weight,
    adapter_down_factors,
    adapter_up_factors,
    slot_adapter,
    adapter_of_block,
    live_rows_of_block,
    prompt_of_block,
    reward_of_block,
):
    rows, window = normed_input_rows.shape
    columns = key_value_cotangent.shape[2]
    dp = lax.axis_size("dp")
    owned = adapter_down_factors.shape[0]
    blocks = reward_of_block.shape[0]
    te = lax.axis_index("tensor")
    chip, core = te // 2, te % 2

    others = [(s, e) for s in (1, 3, 2, 0) for e in (0, 1) if (s, e) != (0, 0)]
    cotangents = [key_value_cotangent]
    slabs = [lax.dynamic_slice_in_dim(key_value_weight, te * window, window, 1)]
    for s, e in others:
        pairs = tensor_pairs(s, e)
        target = ((chip + s) % 4) * 2 + (core + e) % 2
        cotangents.append(lax.ppermute(key_value_cotangent, "tensor", pairs))
        slab = lax.dynamic_slice_in_dim(key_value_weight, target * window, window, 1)
        slabs.append(lax.ppermute(slab, "tensor", pairs))

    part_hi = lax.reduce_precision(reward_of_block, 8, 7)
    rest = reward_of_block - part_hi
    part_mid = lax.reduce_precision(rest, 8, 7)
    part_lo = rest - part_mid
    facts = jnp.concatenate([part_hi, part_mid, part_lo, prompt_of_block.astype(F32)]).astype(BF)
    facts = jnp.pad(facts[None, :], ((0, owned - 1), (0, 128 - 4 * blocks)))
    packed = jnp.concatenate([adapter_down_factors, adapter_up_factors, facts], axis=1)
    packed = jnp.broadcast_to(packed[None], (dp, *packed.shape))
    gathered = lax.all_to_all(packed, "dp", 0, 0)
    a_all = gathered[:, :, :window].reshape(SLOTS * RANK, window)
    b_all = gathered[:, :, window : window + columns].reshape(SLOTS * RANK, columns)
    facts_all = gathered[:, 0, window + columns : window + columns + 4 * blocks].astype(F32)
    facts_all = facts_all.reshape(dp, 4, blocks)
    reward_all = ((facts_all[:, 0] + facts_all[:, 1]) + facts_all[:, 2]).reshape(-1)
    prompt_all = facts_all[:, 3].astype(jnp.int32).reshape(-1)

    member_all = prompt_all[:, None] == jnp.arange(GROUPS, dtype=jnp.int32)[None, :]
    totals = jnp.sum(jnp.where(member_all, reward_all[:, None], 0.0), axis=0)
    squares = jnp.sum(jnp.where(member_all, (reward_all * reward_all)[:, None], 0.0), axis=0)
    mean_g = totals / GSIZE
    spread_g = jnp.sqrt(jnp.maximum(squares / GSIZE - mean_g * mean_g, 1.0))
    member = prompt_of_block[:, None] == jnp.arange(GROUPS, dtype=jnp.int32)[None, :]
    mean_b = jnp.sum(jnp.where(member, mean_g[None, :], 0.0), axis=1)
    spread_b = jnp.sum(jnp.where(member, spread_g[None, :], 0.0), axis=1)
    advantage = (reward_of_block - mean_b) / spread_b
    live = jnp.arange(BLOCK, dtype=jnp.int32)[None, :] < live_rows_of_block[:, None]
    coef = jnp.where(live, -advantage[:, None] / GSIZE, 0.0).reshape(rows, 1)

    value_cotangent = (key_value_cotangent[:, 1, :].astype(F32) * coef).astype(BF)
    chosen = adapter_of_block[:, None] == slot_adapter[None, :]
    chosen = jnp.broadcast_to(chosen[:, None, :], (blocks, BLOCK, SLOTS)).reshape(rows, SLOTS)
    chosen_wide = jnp.broadcast_to(chosen[:, :, None], (rows, SLOTS, RANK)).reshape(
        rows, SLOTS * RANK
    )

    def own_slot(every):
        picked = jnp.where(chosen_wide, every, 0.0)
        return sum(picked[:, k * RANK : (k + 1) * RANK] for k in range(SLOTS))

    low = jnp.concatenate(
        [
            own_slot(dot(normed_input_rows, a_all, 1, 1)),
            own_slot(dot(value_cotangent, b_all, 1, 1)),
        ],
        axis=1,
    )
    low = low + lax.ppermute(low, "tensor", tensor_pairs(0, 1))
    low_sent = low.astype(BF)
    low = low_sent.astype(F32) + sum(
        lax.ppermute(low_sent, "tensor", tensor_pairs(s, 0)).astype(F32) for s in (1, 3, 2)
    )
    low = low.astype(BF)
    spread_low = lambda v: jnp.where(chosen_wide, jnp.tile(v, (1, SLOTS)), jnp.zeros((), BF))
    hidden_wide = spread_low(low[:, :RANK])
    narrow_wide = spread_low(low[:, RANK:])

    terms = jnp.concatenate(
        [
            LOWRANK_MULTIPLIER * dot(narrow_wide, normed_input_rows, 0, 0),
            LOWRANK_MULTIPLIER * dot(hidden_wide, value_cotangent, 0, 0),
        ],
        axis=1,
    ).astype(BF)
    terms = lax.all_to_all(terms.reshape(dp, owned, window + columns), "dp", 0, 0)
    grads = jnp.sum(terms.astype(F32), axis=0)
    grad_a, grad_b = grads[:, :window], grads[:, window:]

    total = LOWRANK_MULTIPLIER * dot(narrow_wide, a_all, 1, 0)
    weighted = jnp.concatenate(cotangents, axis=2).astype(F32) * coef[:, :, None]
    weighted = weighted.astype(BF)
    for i, slab in enumerate(slabs):
        for j in range(2):
            total = total + dot(weighted[:, j, i * columns : (i + 1) * columns], slab[j], 1, 1)
    return (total.astype(BF), grad_a, grad_b)


def solution(mesh):
    in_specs = (
        P("dp", "tensor"),
        P("dp", None, "tensor"),
        P(None, None, "tensor"),
        P("dp", "tensor"),
        P("dp", "tensor"),
        P(),
        P("dp"),
        P("dp"),
        P("dp"),
        P("dp"),
    )
    out_specs = (P("dp", "tensor"), P("dp", "tensor"), P("dp", "tensor"))
    return jax.shard_map(shards, mesh=mesh, in_specs=in_specs, out_specs=out_specs, check_vma=False)
```

```python
import jax
import jax.numpy as jnp
from jax import lax
from jax.experimental import pallas as pl
from jax.experimental.pallas import tpu as pltpu
from jax.sharding import PartitionSpec as P

BLOCK = 128
GSIZE = 8
GROUPS = 16
SLOTS = 8
RANK = 64
CHIP_STEPS = (1, 3, 2)
LOWRANK_MULTIPLIER = 2.0
BF = jnp.bfloat16
F32 = jnp.float32


def tensor_pairs(chip_step, core_flip):
    return [
        (y * 2 + c, ((y + chip_step) % 4) * 2 + (c ^ core_flip)) for y in range(4) for c in range(2)
    ]


def dot(a, b, ca, cb):
    return lax.dot_general(a, b, (((ca,), (cb,)), ((), ())), preferred_element_type=F32)


def frozen_kernel(place, same_ref, other_ref, *refs):
    *slab_refs, narrow_ref, a_ref, coef_ref, out_ref, weighted = refs
    chips, _, rows, columns = same_ref.shape

    @pl.when(pl.program_id(0) == 0)
    def _():
        coef = coef_ref[...]
        for half, ref in enumerate((same_ref, other_ref)):
            for i in range(chips):
                for j in range(2):
                    k = ((half * chips + i) * 2 + j) * columns
                    weighted[:, k : k + columns] = (ref[i, j].astype(F32) * coef).astype(BF)

    slabs = [ref[j] for ref in slab_refs for j in range(2)]
    total = dot(weighted[...], jnp.concatenate(slabs, axis=1), 1, 1)
    total = total + LOWRANK_MULTIPLIER * dot(narrow_ref[...], a_ref[...], 1, 0)
    out_ref[...] = total.astype(BF)


def frozen_and_correction(te, same_core, other_core, weight, arrived, narrow, a_all, coef):
    _, window, columns = arrived[0].shape
    chips, _, rows, _ = same_core.shape
    depth = narrow.shape[1]
    tile = 256
    steps = window // tile
    resident = lambda shape: pl.BlockSpec(shape, lambda i, p: (0,) * len(shape))
    return pl.pallas_call(
        frozen_kernel,
        grid_spec=pltpu.PrefetchScalarGridSpec(
            num_scalar_prefetch=1,
            grid=(steps,),
            in_specs=[
                resident((chips, 2, rows, columns)),
                resident((chips, 2, rows, columns)),
                pl.BlockSpec((2, tile, columns), lambda i, p: (0, p[0] * steps + i, 0)),
                *[pl.BlockSpec((2, tile, columns), lambda i, p: (0, i, 0)) for _ in arrived],
                resident((rows, depth)),
                pl.BlockSpec((depth, tile), lambda i, p: (0, i)),
                resident((rows, 1)),
            ],
            out_specs=pl.BlockSpec((rows, tile), lambda i, p: (0, i)),
            scratch_shapes=[pltpu.VMEM((rows, 4 * chips * columns), BF)],
        ),
        out_shape=jax.ShapeDtypeStruct((rows, window), BF),
        compiler_params=pltpu.CompilerParams(vmem_limit_bytes=32 * 2**20),
        cost_estimate=pl.CostEstimate(
            flops=2 * rows * window * (4 * chips * columns + depth),
            bytes_accessed=8 * 2**20,
            transcendentals=0,
        ),
    )(te.reshape(1), same_core, other_core, weight, *arrived, narrow, a_all, coef)


def shards(
    normed_input_rows,
    key_value_cotangent,
    key_value_weight,
    adapter_down_factors,
    adapter_up_factors,
    slot_adapter,
    adapter_of_block,
    live_rows_of_block,
    prompt_of_block,
    reward_of_block,
):
    rows, window = normed_input_rows.shape
    columns = key_value_cotangent.shape[2]
    dp = lax.axis_size("dp")
    owned = adapter_down_factors.shape[0]
    blocks = reward_of_block.shape[0]
    te = lax.axis_index("tensor")
    chip, core = te // 2, te % 2

    def slab_for(chip_step, core_flip):
        target = ((chip + chip_step) % 4) * 2 + (core + core_flip) % 2
        return lax.dynamic_slice_in_dim(key_value_weight, target * window, window, 1)

    def send(value, chip_step, core_flip):
        return lax.ppermute(value, "tensor", tensor_pairs(chip_step, core_flip))

    cotangent = jnp.transpose(key_value_cotangent, (1, 0, 2))
    cotangents = [cotangent] + [send(cotangent, s, 0) for s in CHIP_STEPS]
    slabs = {(s, 0): send(slab_for(s, 0), s, 0) for s in (1, 3)}
    relayed = [send(slab_for(2, 0), 1, 0), send(slab_for(2, 1), 3, 1)]

    part_hi = lax.reduce_precision(reward_of_block, 8, 7)
    rest = reward_of_block - part_hi
    part_mid = lax.reduce_precision(rest, 8, 7)
    part_lo = rest - part_mid
    facts = jnp.concatenate([part_hi, part_mid, part_lo, prompt_of_block.astype(F32)]).astype(BF)
    facts = jnp.pad(facts[None, :], ((0, owned - 1), (0, 128 - 4 * blocks)))
    packed = jnp.concatenate([adapter_down_factors, adapter_up_factors, facts], axis=1)
    packed = jnp.broadcast_to(packed[None], (dp, *packed.shape))
    gathered = lax.all_to_all(packed, "dp", 0, 0)
    gathered, cotangents, slabs = lax.optimization_barrier((gathered, cotangents, slabs))
    a_all = gathered[:, :, :window].reshape(SLOTS * RANK, window)
    b_all = gathered[:, :, window : window + columns].reshape(SLOTS * RANK, columns)
    facts_all = gathered[:, 0, window + columns : window + columns + 4 * blocks].astype(F32)
    facts_all = facts_all.reshape(dp, 4, blocks)
    reward_all = ((facts_all[:, 0] + facts_all[:, 1]) + facts_all[:, 2]).reshape(-1)
    prompt_all = facts_all[:, 3].astype(jnp.int32).reshape(-1)

    member_all = prompt_all[:, None] == jnp.arange(GROUPS, dtype=jnp.int32)[None, :]
    totals = jnp.sum(jnp.where(member_all, reward_all[:, None], 0.0), axis=0)
    squares = jnp.sum(jnp.where(member_all, (reward_all * reward_all)[:, None], 0.0), axis=0)
    mean_g = totals / GSIZE
    spread_g = jnp.sqrt(jnp.maximum(squares / GSIZE - mean_g * mean_g, 1.0))
    member = prompt_of_block[:, None] == jnp.arange(GROUPS, dtype=jnp.int32)[None, :]
    mean_b = jnp.sum(jnp.where(member, mean_g[None, :], 0.0), axis=1)
    spread_b = jnp.sum(jnp.where(member, spread_g[None, :], 0.0), axis=1)
    advantage = (reward_of_block - mean_b) / spread_b
    live = jnp.arange(BLOCK, dtype=jnp.int32)[None, :] < live_rows_of_block[:, None]
    coef = jnp.where(live, -advantage[:, None] / GSIZE, 0.0).reshape(rows, 1)

    value_cotangent = (key_value_cotangent[:, 1, :].astype(F32) * coef).astype(BF)
    chosen = adapter_of_block[:, None] == slot_adapter[None, :]
    chosen = jnp.broadcast_to(chosen[:, None, :], (blocks, BLOCK, SLOTS)).reshape(rows, SLOTS)
    chosen_wide = jnp.broadcast_to(chosen[:, :, None], (rows, SLOTS, RANK)).reshape(
        rows, SLOTS * RANK
    )

    def own_slot(every):
        picked = jnp.where(chosen_wide, every, 0.0)
        return sum(picked[:, k * RANK : (k + 1) * RANK] for k in range(SLOTS))

    low = jnp.concatenate(
        [
            own_slot(dot(normed_input_rows, a_all, 1, 1)),
            own_slot(dot(value_cotangent, b_all, 1, 1)),
        ],
        axis=1,
    )
    low = low + lax.ppermute(low, "tensor", tensor_pairs(0, 1))
    low_sent = low.astype(BF)
    low = low_sent.astype(F32) + sum(
        lax.ppermute(low_sent, "tensor", tensor_pairs(s, 0)).astype(F32) for s in CHIP_STEPS
    )
    low = low.astype(BF)
    spread_low = lambda v: jnp.where(chosen_wide, jnp.tile(v, (1, SLOTS)), jnp.zeros((), BF))
    hidden_wide = spread_low(low[:, :RANK])
    narrow_wide = spread_low(low[:, RANK:])

    terms = jnp.concatenate(
        [
            LOWRANK_MULTIPLIER * dot(narrow_wide, normed_input_rows, 0, 0),
            LOWRANK_MULTIPLIER * dot(hidden_wide, value_cotangent, 0, 0),
        ],
        axis=1,
    ).astype(BF)
    terms, relayed = lax.optimization_barrier((terms, relayed))
    terms = lax.all_to_all(terms.reshape(dp, owned, window + columns), "dp", 0, 0)
    grad_a = jnp.sum(terms[:, :, :window].astype(F32), axis=0)
    grad_b = jnp.sum(terms[:, :, window:].astype(F32), axis=0)

    same_core = jnp.stack(cotangents)
    other_core = send(same_core, 0, 1)
    slabs[(2, 0)] = send(relayed[0], 1, 0)
    slabs[(2, 1)] = send(relayed[1], 3, 0)
    slabs |= {(s, 1): send(slab_for(s, 1), s, 1) for s in (1, 3, 0)}
    arrived = [slabs[(s, e)] for e in (0, 1) for s in (0, *CHIP_STEPS) if (s, e) != (0, 0)]
    input_gradient = frozen_and_correction(
        te, same_core, other_core, key_value_weight, arrived, narrow_wide, a_all, coef
    )
    return (input_gradient, grad_a, grad_b)


def solution(mesh):
    in_specs = (
        P("dp", "tensor"),
        P("dp", None, "tensor"),
        P(None, None, "tensor"),
        P("dp", "tensor"),
        P("dp", "tensor"),
        P(),
        P("dp"),
        P("dp"),
        P("dp"),
        P("dp"),
    )
    out_specs = (P("dp", "tensor"), P("dp", "tensor"), P("dp", "tensor"))
    return jax.shard_map(shards, mesh=mesh, in_specs=in_specs, out_specs=out_specs, check_vma=False)
```

```python
import jax
import jax.numpy as jnp
from jax import lax
from jax.experimental import pallas as pl
from jax.experimental.pallas import tpu as pltpu
from jax.sharding import PartitionSpec as P

BLOCK = 128
GSIZE = 8
SLOTS = 8
RANK = 64
LANES = 128
CHIPS = 4
LOWRANK_MULTIPLIER = 2.0
BF = jnp.bfloat16
F32 = jnp.float32
VMEM = pl.BlockSpec(memory_space=pltpu.VMEM)
SMEM = pl.BlockSpec(memory_space=pltpu.SMEM)


def dot(a, b, ca, cb):
    return lax.dot_general(a, b, (((ca,), (cb,)), ((), ())), preferred_element_type=F32)


def call(kernel, in_specs, shapes, flops, mib):
    single = not isinstance(shapes, (list, tuple))
    shapes = [shapes] if single else list(shapes)
    return pl.pallas_call(
        kernel,
        in_specs=in_specs,
        out_specs=VMEM if single else [VMEM] * len(shapes),
        out_shape=shapes[0] if single else shapes,
        compiler_params=pltpu.CompilerParams(vmem_limit_bytes=mib * 2**20),
        cost_estimate=pl.CostEstimate(flops=flops, bytes_accessed=2**20, transcendentals=0),
    )


def tensor_send(value, chip_step, core_flip):
    pairs = [
        (y * 2 + c, (y + chip_step) % CHIPS * 2 + (c ^ core_flip))
        for y in range(CHIPS)
        for c in range(2)
    ]
    return lax.ppermute(value, "tensor", pairs)


def x_send(value, step):
    pairs = [(i, i // 4 * 4 + (i + step) % 4) for i in range(lax.axis_size("dp"))]
    return lax.ppermute(value, "dp", pairs)


def pack_kernel(prompt, reward, down_ref, up_ref, out_ref):
    shape = (down_ref.shape[0], LANES)
    row = lax.broadcasted_iota(jnp.int32, shape, 0)
    lane = lax.broadcasted_iota(jnp.int32, shape, 1)
    blocks = reward.shape[0]
    rewards = jnp.zeros(shape, F32)
    prompts = jnp.full(shape, -1.0, F32)
    for b in range(blocks):
        rewards = jnp.where(lane % blocks == b, reward[b], rewards)
        prompts = jnp.where(lane == b, prompt[b].astype(F32), prompts)
    high = rewards.astype(BF).astype(F32)
    rest = rewards - high
    middle = rest.astype(BF).astype(F32)
    part = lane // blocks
    parts = jnp.where(part == 0, high, jnp.where(part == 1, middle, rest - middle))
    parts = jnp.where(part < 3, parts, 0.0)
    facts = jnp.where(row == 0, parts, jnp.where(row == 1, prompts, 0.0)).astype(BF)
    packed = jnp.concatenate([down_ref[...], up_ref[...], facts], axis=1)
    for i in range(out_ref.shape[0]):
        out_ref[i] = packed


def factor_rows(ref, slot, start, size):
    owners = ref.shape[0] // SLOTS
    return ref[pl.ds(slot * owners, owners), :, pl.ds(start, size)].reshape(RANK, size)


def low_kernel(
    slots, live, prompt, reward, gathered_ref, x_ref, cot_ref, low_ref, weighted_ref, coef_ref
):
    window = x_ref.shape[1]
    columns = cot_ref.shape[2]
    blocks = reward.shape[0]
    facts = gathered_ref[:, :, window + columns :].astype(F32)
    row = lax.broadcasted_iota(jnp.int32, facts.shape, 1)
    parts = jnp.sum(jnp.where(row == 0, facts, 0.0), axis=1)
    prompts = jnp.sum(jnp.where(row == 1, facts, 0.0), axis=1)
    rewards = parts + pltpu.roll(parts, LANES - blocks, 1)
    rewards = rewards + pltpu.roll(parts, LANES - 2 * blocks, 1)
    place = lax.broadcasted_iota(jnp.int32, (BLOCK, 1), 0)
    whole = lambda v: jnp.sum(jnp.sum(v, axis=1, keepdims=True), axis=0, keepdims=True)
    for b in range(blocks):
        same = prompts == prompt[b].astype(F32)
        mean = whole(jnp.where(same, rewards, 0.0)) / GSIZE
        square = whole(jnp.where(same, rewards * rewards, 0.0)) / GSIZE
        spread = jnp.sqrt(jnp.maximum(square - mean * mean, 1.0))
        advantage = (reward[b] - mean) / spread
        coef = jnp.where(place < live[b], -advantage / GSIZE, 0.0)
        rows = pl.ds(b * BLOCK, BLOCK)
        weighted = (cot_ref[1, rows, :].astype(F32) * coef).astype(BF)
        low_h = dot(x_ref[rows, :], factor_rows(gathered_ref, slots[b], 0, window), 1, 1)
        low_g = dot(weighted, factor_rows(gathered_ref, slots[b], window, columns), 1, 1)
        low_ref[rows, :] = jnp.concatenate([low_h, low_g], axis=1)
        weighted_ref[rows, :] = weighted
        coef_ref[rows, :] = coef


def terms_kernel(slots, own, first, second, third, x_ref, weighted_ref, terms_ref, low_ref):
    window = x_ref.shape[1]
    columns = weighted_ref.shape[1]
    owners, owned = terms_ref.shape[0] // SLOTS, terms_ref.shape[1]
    low = own[...].astype(F32) + first[...].astype(F32)
    low = (low + second[...].astype(F32)) + third[...].astype(F32)
    low_ref[...] = low.astype(BF)
    for i in range(terms_ref.shape[0]):
        terms_ref[i] = jnp.zeros(terms_ref.shape[1:], BF)
    for b in range(x_ref.shape[0] // BLOCK):
        rows = pl.ds(b * BLOCK, BLOCK)
        low = low_ref[rows, :]
        down = LOWRANK_MULTIPLIER * dot(low, x_ref[rows, :], 0, 0)[RANK:]
        up = LOWRANK_MULTIPLIER * dot(low, weighted_ref[rows, :], 0, 0)[:RANK]
        place = pl.ds(slots[b] * owners, owners)
        terms_ref[place, :, :window] = down.astype(BF).reshape(owners, owned, window)
        terms_ref[place, :, window:] = up.astype(BF).reshape(owners, owned, columns)


def frozen_kernel(slots, quarters, *refs):
    *cot_refs, gathered_ref, low_ref, coef_ref, w0, w1, w2, w3a, w3b, out_ref, weighted = refs
    tile = w0.shape[2]
    columns = w0.shape[3]
    coef = coef_ref[...]
    at = 0
    for ref in cot_refs:
        for i in range(ref.shape[0] // 2):
            for j in range(2):
                both = ref[2 * i + j].astype(F32) * coef
                weighted[:, at : at + columns] = both.astype(BF)
                at += columns
    for r, parts in enumerate(((w0,), (w1,), (w2,), (w3a, w3b))):
        slabs = [p[i, j] for p in parts for i in range(p.shape[0]) for j in range(2)]
        total = dot(weighted[...], jnp.concatenate(slabs, axis=1), 1, 1)
        start = pl.multiple_of(quarters[r] * tile, tile)
        for b in range(total.shape[0] // BLOCK):
            rows = slice(b * BLOCK, (b + 1) * BLOCK)
            factor = factor_rows(gathered_ref, slots[b], start, tile)
            factor = jnp.concatenate([jnp.zeros_like(factor), factor], axis=0)
            extra = LOWRANK_MULTIPLIER * dot(low_ref[rows, :], factor, 1, 0)
            out_ref[rows, pl.ds(start, tile)] = (total[rows] + extra).astype(BF)


def sum_kernel(terms_ref, down_ref, up_ref):
    window = down_ref.shape[1]
    total = terms_ref[0].astype(F32)
    for i in range(1, terms_ref.shape[0]):
        total = total + terms_ref[i].astype(F32)
    down_ref[...] = total[:, :window]
    up_ref[...] = total[:, window:]


def shards(
    normed_input_rows,
    key_value_cotangent,
    key_value_weight,
    adapter_down_factors,
    adapter_up_factors,
    slot_adapter,
    adapter_of_block,
    live_rows_of_block,
    prompt_of_block,
    reward_of_block,
):
    rows, window = normed_input_rows.shape
    columns = key_value_cotangent.shape[2]
    dp = lax.axis_size("dp")
    owned = adapter_down_factors.shape[0]
    te = lax.axis_index("tensor")
    chip, core = te // 2, te % 2
    x = lax.axis_index("dp") % 4
    tile = window // 4
    shape = jax.ShapeDtypeStruct
    slots = jnp.sum(
        jnp.where(
            adapter_of_block[:, None] == slot_adapter[None, :], jnp.arange(SLOTS, dtype=jnp.int32), 0
        ),
        axis=1,
    )

    packed = call(
        pack_kernel, [SMEM, SMEM, VMEM, VMEM], shape((dp, owned, window + columns + LANES), BF), 0, 8
    )(prompt_of_block, reward_of_block, adapter_down_factors, adapter_up_factors)
    gathered = lax.all_to_all(packed, "dp", 0, 0)

    def quarter(chip_step, core_flip):
        target = ((chip + chip_step) % CHIPS) * 2 + (core + core_flip) % 2
        start = target * window + x * tile
        return lax.dynamic_slice_in_dim(key_value_weight, start, tile, 1)

    before = tensor_send(jnp.stack([quarter(1, 0), quarter(1, 1), quarter(2, 0)]), 1, 0)
    after = tensor_send(jnp.stack([quarter(3, 0), quarter(3, 1), quarter(2, 1)]), 3, 0)
    across = tensor_send(before[2], 1, 0)
    across_other = tensor_send(after[2], 3, 0)
    other = jnp.stack([quarter(0, 1), before[1], after[1], across_other])
    slabs = jnp.concatenate(
        [jnp.stack([quarter(0, 0), before[0], after[0], across]), tensor_send(other, 0, 1)]
    )
    gathered, slabs = lax.optimization_barrier((gathered, slabs))

    cotangent = jnp.transpose(key_value_cotangent, (1, 0, 2))
    low, weighted_value, coef = call(
        low_kernel,
        [SMEM] * 4 + [VMEM] * 3,
        [shape((rows, 2 * RANK), F32), shape((rows, columns), BF), shape((rows, 1), F32)],
        2 * rows * RANK * window,
        16,
    )(
        slots,
        live_rows_of_block,
        prompt_of_block,
        reward_of_block,
        gathered,
        normed_input_rows,
        cotangent,
    )
    low = (low + tensor_send(low, 0, 1)).astype(BF)
    lows = [low] + [tensor_send(low, s, 0) for s in (1, 3, 2)]
    slabs_left, slabs_right = x_send(slabs, 1), x_send(slabs, 3)

    terms, low = call(
        terms_kernel,
        [SMEM] + [VMEM] * 6,
        [shape((dp, owned, window + columns), BF), shape((rows, 2 * RANK), BF)],
        4 * rows * RANK * window,
        16,
    )(slots, *lows, normed_input_rows, weighted_value)
    terms, slabs_left, slabs_right = lax.optimization_barrier((terms, slabs_left, slabs_right))
    terms = lax.all_to_all(terms, "dp", 0, 0)

    slabs_far = (x_send(slabs_left[:4], 1), x_send(slabs_right[4:], 3))
    cot_before, cot_after = tensor_send(cotangent, 1, 0), tensor_send(cotangent, 3, 0)
    relay = [(y * 2 + c, (y + 1 + 2 * c) % CHIPS * 2 + c) for y in range(CHIPS) for c in range(2)]
    cot_across = lax.ppermute(jnp.where(core == 0, cot_before, cot_after), "tensor", relay)
    cots = jnp.concatenate([cotangent, cot_before, cot_after, cot_across])
    cots_other = tensor_send(cots, 0, 1)
    quarters = (x + jnp.array([0, 3, 1, 2], jnp.int32)) % 4
    input_gradient = pl.pallas_call(
        frozen_kernel,
        in_specs=[SMEM] * 2 + [VMEM] * 10,
        out_specs=VMEM,
        out_shape=shape((rows, window), BF),
        scratch_shapes=[pltpu.VMEM((rows, 16 * columns), BF)],
        compiler_params=pltpu.CompilerParams(vmem_limit_bytes=28 * 2**20),
        cost_estimate=pl.CostEstimate(
            flops=2 * rows * window * 18 * columns, bytes_accessed=8 * 2**20, transcendentals=0
        ),
    )(
        slots,
        quarters,
        cots,
        cots_other,
        gathered,
        low,
        coef,
        slabs,
        slabs_left,
        slabs_right,
        *slabs_far,
    )
    grad_a, grad_b = call(
        sum_kernel,
        [VMEM],
        [shape((owned, window), F32), shape((owned, columns), F32)],
        0,
        8,
    )(terms)
    return (input_gradient, grad_a, grad_b)


def solution(mesh):
    in_specs = (
        P("dp", "tensor"),
        P("dp", None, "tensor"),
        P(None, None, "tensor"),
        P("dp", "tensor"),
        P("dp", "tensor"),
        P(),
        P("dp"),
        P("dp"),
        P("dp"),
        P("dp"),
    )
    out_specs = (P("dp", "tensor"), P("dp", "tensor"), P("dp", "tensor"))
    return jax.shard_map(shards, mesh=mesh, in_specs=in_specs, out_specs=out_specs, check_vma=False)
```

```python
import jax
import jax.numpy as jnp
from jax import lax
from jax.experimental import pallas as pl
from jax.experimental.pallas import tpu as pltpu
from jax.sharding import PartitionSpec as P

BLOCK = 128
GSIZE = 8
SLOTS = 8
RANK = 64
LANES = 128
CHIPS = 4
FULL_VMEM = 60 * 2**20
LOWRANK_MULTIPLIER = 2.0
BF = jnp.bfloat16
F32 = jnp.float32
VMEM = pl.BlockSpec(memory_space=pltpu.VMEM)
SMEM = pl.BlockSpec(memory_space=pltpu.SMEM)


def dot(a, b, ca, cb):
    return lax.dot_general(a, b, (((ca,), (cb,)), ((), ())), preferred_element_type=F32)


def call(kernel, in_specs, shapes, flops, mib):
    single = not isinstance(shapes, (list, tuple))
    shapes = [shapes] if single else list(shapes)
    return pl.pallas_call(
        kernel,
        in_specs=in_specs,
        out_specs=VMEM if single else [VMEM] * len(shapes),
        out_shape=shapes[0] if single else shapes,
        compiler_params=pltpu.CompilerParams(vmem_limit_bytes=mib * 2**20),
        cost_estimate=pl.CostEstimate(flops=flops, bytes_accessed=2**20, transcendentals=0),
    )


def tensor_send(value, chip_step, core_flip):
    pairs = [
        (y * 2 + c, (y + chip_step) % CHIPS * 2 + (c ^ core_flip))
        for y in range(CHIPS)
        for c in range(2)
    ]
    return lax.ppermute(value, "tensor", pairs)


def x_send(value, step):
    pairs = [(i, i // 4 * 4 + (i + step) % 4) for i in range(lax.axis_size("dp"))]
    return lax.ppermute(value, "dp", pairs)


def pack_kernel(prompt, reward, down_ref, up_ref, out_ref):
    shape = (down_ref.shape[0], LANES)
    row = lax.broadcasted_iota(jnp.int32, shape, 0)
    lane = lax.broadcasted_iota(jnp.int32, shape, 1)
    blocks = reward.shape[1]
    rewards = jnp.zeros(shape, F32)
    prompts = jnp.full(shape, -1.0, F32)
    for b in range(blocks):
        one = (slice(0, 1), slice(b, b + 1))
        rewards = jnp.where(lane % blocks == b, reward[one], rewards)
        prompts = jnp.where(lane == b, prompt[one].astype(F32), prompts)
    high = rewards.astype(BF).astype(F32)
    rest = rewards - high
    middle = rest.astype(BF).astype(F32)
    part = lane // blocks
    parts = jnp.where(part == 0, high, jnp.where(part == 1, middle, rest - middle))
    parts = jnp.where(part < 3, parts, 0.0)
    facts = jnp.where(row == 0, parts, jnp.where(row == 1, prompts, 0.0)).astype(BF)
    packed = jnp.concatenate([down_ref[...], up_ref[...], facts], axis=1)
    for i in range(out_ref.shape[0]):
        out_ref[i] = packed


def streamed(kernel, blocks, out):
    whole = lambda shape: pl.BlockSpec(shape, lambda i: (0,) * len(shape))
    return pl.pallas_call(
        kernel,
        grid=(1,),
        in_specs=[whole(shape) for shape in blocks],
        out_specs=whole(out),
        out_shape=jax.ShapeDtypeStruct(out, BF),
        compiler_params=pltpu.CompilerParams(vmem_limit_bytes=FULL_VMEM),
    )


def payload_kernel(places, *refs):
    *slabs, cot_ref, next_ref, next_other, prev_ref, prev_other, mine_ref, other_ref = refs
    tile, rows = slabs[0].shape[1], cot_ref.shape[1]
    key, value = (cot_ref.at[0],), (cot_ref.at[1],)
    slab = lambda i: (slabs[i].at[0], slabs[i].at[1])
    orders = (
        (next_ref, (slab(0), slab(2), key, value)),
        (next_other, (slab(1),)),
        (prev_ref, (slab(3), key, value, slab(5))),
        (prev_other, (slab(4),)),
        (mine_ref, (slab(6),)),
        (other_ref, (slab(7),)),
    )
    for out_ref, units in orders:
        at = 0
        for piece in (p for unit in units for p in unit):
            out_ref[at : at + piece.shape[0]] = piece[...]
            at += piece.shape[0]


def payloads(places, weight, cotangent, tile):
    columns = weight.shape[2]
    slab = [
        pl.BlockSpec((2, tile, columns), lambda g, p, i=i: (0, p[i], 0)) for i in range(8)
    ]
    sizes = [n * 2 * tile for n in (4, 1, 4, 1, 1, 1)]
    return pl.pallas_call(
        payload_kernel,
        grid_spec=pltpu.PrefetchScalarGridSpec(
            num_scalar_prefetch=1,
            grid=(1,),
            in_specs=[*slab, pl.BlockSpec(cotangent.shape, lambda g, p: (0, 0, 0))],
            out_specs=[pl.BlockSpec((n, columns), lambda g, p: (0, 0)) for n in sizes],
        ),
        out_shape=[jax.ShapeDtypeStruct((n, columns), BF) for n in sizes],
        compiler_params=pltpu.CompilerParams(vmem_limit_bytes=FULL_VMEM),
    )(places, *[weight] * 8, cotangent)


def factor_rows(ref, slot, start, size):
    owners = ref.shape[0] // SLOTS
    return ref[pl.ds(slot * owners, owners), :, pl.ds(start, size)].reshape(RANK, size)


def low_kernel(
    slots, live, prompt, reward, gathered_ref, x_ref, cot_ref, low_ref, weighted_ref, coef_ref
):
    window = x_ref.shape[1]
    columns = cot_ref.shape[2]
    blocks = reward.shape[0]
    facts = gathered_ref[:, :, window + columns :].astype(F32)
    row = lax.broadcasted_iota(jnp.int32, facts.shape, 1)
    parts = jnp.sum(jnp.where(row == 0, facts, 0.0), axis=1)
    prompts = jnp.sum(jnp.where(row == 1, facts, 0.0), axis=1)
    rewards = parts + pltpu.roll(parts, LANES - blocks, 1)
    rewards = rewards + pltpu.roll(parts, LANES - 2 * blocks, 1)
    place = lax.broadcasted_iota(jnp.int32, (BLOCK, 1), 0)
    whole = lambda v: jnp.sum(jnp.sum(v, axis=1, keepdims=True), axis=0, keepdims=True)
    for b in range(blocks):
        same = prompts == prompt[b].astype(F32)
        mean = whole(jnp.where(same, rewards, 0.0)) / GSIZE
        square = whole(jnp.where(same, rewards * rewards, 0.0)) / GSIZE
        spread = jnp.sqrt(jnp.maximum(square - mean * mean, 1.0))
        advantage = (reward[b] - mean) / spread
        coef = jnp.where(place < live[b], -advantage / GSIZE, 0.0)
        rows = pl.ds(b * BLOCK, BLOCK)
        weighted = (cot_ref[1, rows, :].astype(F32) * coef).astype(BF)
        low_h = dot(x_ref[rows, :], factor_rows(gathered_ref, slots[b], 0, window), 1, 1)
        low_g = dot(weighted, factor_rows(gathered_ref, slots[b], window, columns), 1, 1)
        low_ref[rows, :] = jnp.concatenate([low_h, low_g], axis=1)
        weighted_ref[rows, :] = weighted
        coef_ref[rows, :] = coef


def terms_kernel(slots, own, first, second, third, x_ref, weighted_ref, terms_ref, low_ref):
    window = x_ref.shape[1]
    columns = weighted_ref.shape[1]
    owners, owned = terms_ref.shape[0] // SLOTS, terms_ref.shape[1]
    low = own[...].astype(F32) + first[...].astype(F32)
    low = (low + second[...].astype(F32)) + third[...].astype(F32)
    low_ref[...] = low.astype(BF)
    for i in range(terms_ref.shape[0]):
        terms_ref[i] = jnp.zeros(terms_ref.shape[1:], BF)
    for b in range(x_ref.shape[0] // BLOCK):
        rows = pl.ds(b * BLOCK, BLOCK)
        low = low_ref[rows, :]
        down = LOWRANK_MULTIPLIER * dot(low, x_ref[rows, :], 0, 0)[RANK:]
        up = LOWRANK_MULTIPLIER * dot(low, weighted_ref[rows, :], 0, 0)[:RANK]
        place = pl.ds(slots[b] * owners, owners)
        terms_ref[place, :, :window] = down.astype(BF).reshape(owners, owned, window)
        terms_ref[place, :, window:] = up.astype(BF).reshape(owners, owned, columns)


def frozen_kernel(slots, quarters, *refs):
    own, before, after, hop_next, hop_prev, swapped, *refs = refs
    gathered_ref, low_ref, coef_ref, w0, w1, w2, w3a, w3b, out_ref, weighted = refs
    rows, columns = own.shape[1:]
    tile = rows // 2
    coef = coef_ref[...]
    pieces = [own.at[0], own.at[1]]
    pieces += [before.at[pl.ds(i * rows, rows)] for i in (2, 3)]
    pieces += [after.at[pl.ds(i * rows, rows)] for i in (1, 2)]
    pieces += [hop_next.at[pl.ds(rows, rows)], swapped.at[pl.ds(7 * rows, rows)]]
    pieces += [swapped.at[pl.ds(i * rows, rows)] for i in range(7)]
    pieces += [hop_prev.at[pl.ds(0, rows)]]
    for i, piece in enumerate(pieces):
        weighted[:, i * columns : (i + 1) * columns] = (piece[...].astype(F32) * coef).astype(BF)
    for r, parts in enumerate(((w0,), (w1,), (w2,), (w3a, w3b))):
        slabs = [
            p[i * tile : (i + 1) * tile] for p in parts for i in range(p.shape[0] // tile)
        ]
        total = dot(weighted[...], jnp.concatenate(slabs, axis=1), 1, 1)
        start = pl.multiple_of(quarters[r] * tile, tile)
        for b in range(rows // BLOCK):
            block = slice(b * BLOCK, (b + 1) * BLOCK)
            factor = factor_rows(gathered_ref, slots[b], start, tile)
            factor = jnp.concatenate([jnp.zeros_like(factor), factor], axis=0)
            extra = LOWRANK_MULTIPLIER * dot(low_ref[block, :], factor, 1, 0)
            out_ref[block, pl.ds(start, tile)] = (total[block] + extra).astype(BF)


def sum_kernel(terms_ref, down_ref, up_ref):
    window = down_ref.shape[1]
    total = terms_ref[0].astype(F32)
    for i in range(1, terms_ref.shape[0]):
        total = total + terms_ref[i].astype(F32)
    down_ref[...] = total[:, :window]
    up_ref[...] = total[:, window:]


def shards(
    normed_input_rows,
    key_value_cotangent,
    key_value_weight,
    adapter_down_factors,
    adapter_up_factors,
    slot_adapter,
    adapter_of_block,
    live_rows_of_block,
    prompt_of_block,
    reward_of_block,
):
    rows, window = normed_input_rows.shape
    columns = key_value_cotangent.shape[2]
    dp = lax.axis_size("dp")
    owned = adapter_down_factors.shape[0]
    te = lax.axis_index("tensor")
    chip, core = te // 2, te % 2
    x = lax.axis_index("dp") % 4
    tile = window // 4
    shape = jax.ShapeDtypeStruct
    slots = jnp.sum(
        jnp.where(
            adapter_of_block[:, None] == slot_adapter[None, :], jnp.arange(SLOTS, dtype=jnp.int32), 0
        ),
        axis=1,
    )

    packed = streamed(
        pack_kernel,
        [(1, 4), (1, 4), (owned, window), (owned, columns)],
        (dp, owned, window + columns + LANES),
    )(
        prompt_of_block.reshape(1, -1),
        reward_of_block.reshape(1, -1),
        adapter_down_factors,
        adapter_up_factors,
    )
    gathered = lax.all_to_all(packed, "dp", 0, 0)

    cotangent = jnp.transpose(key_value_cotangent, (1, 0, 2))
    steps = jnp.array([[1, 0], [1, 1], [2, 0], [3, 0], [3, 1], [2, 1], [0, 0], [0, 1]], jnp.int32)
    targets = (chip + steps[:, 0]) % CHIPS * 2 + (core + steps[:, 1]) % 2
    to_next, next_other, to_prev, prev_other, mine, other = payloads(
        targets * 4 + x, key_value_weight, cotangent, tile
    )
    before, after = tensor_send(to_next, 1, 0), tensor_send(to_prev, 3, 0)
    before_other, after_other = tensor_send(next_other, 1, 1), tensor_send(prev_other, 3, 1)
    partner = tensor_send(other, 0, 1)
    unit = 2 * tile
    part = lambda v, start, stop: v[start * unit : stop * unit]
    hop_next, hop_prev = lax.optimization_barrier((part(before, 1, 3), part(after, 2, 4)))
    hop_next, hop_prev = tensor_send(hop_next, 1, 0), tensor_send(hop_prev, 3, 1)
    slabs = jnp.concatenate(
        [
            mine,
            part(before, 0, 1),
            part(after, 0, 1),
            part(hop_next, 0, 1),
            partner,
            before_other,
            after_other,
            part(hop_prev, 1, 2),
        ]
    )
    gathered, slabs, hop_next, hop_prev = lax.optimization_barrier(
        (gathered, slabs, hop_next, hop_prev)
    )

    low, weighted_value, coef = call(
        low_kernel,
        [SMEM] * 4 + [VMEM] * 3,
        [shape((rows, 2 * RANK), F32), shape((rows, columns), BF), shape((rows, 1), F32)],
        2 * rows * RANK * window,
        16,
    )(
        slots,
        live_rows_of_block,
        prompt_of_block,
        reward_of_block,
        gathered,
        normed_input_rows,
        cotangent,
    )
    low = (low + tensor_send(low, 0, 1)).astype(BF)
    lows = [low] + [tensor_send(low, s, 0) for s in (1, 3, 2)]
    slabs_left, slabs_right = x_send(slabs, 1), x_send(slabs, 3)

    terms, low = call(
        terms_kernel,
        [SMEM] + [VMEM] * 6,
        [shape((dp, owned, window + columns), BF), shape((rows, 2 * RANK), BF)],
        4 * rows * RANK * window,
        16,
    )(slots, *lows, normed_input_rows, weighted_value)
    terms, slabs_left, slabs_right = lax.optimization_barrier((terms, slabs_left, slabs_right))
    terms = lax.all_to_all(terms, "dp", 0, 0)
    swapped = jnp.concatenate(
        [
            cotangent.reshape(2 * rows, columns),
            part(before, 2, 4),
            part(after, 1, 3),
            part(hop_next, 1, 2),
            part(hop_prev, 0, 1),
        ]
    )
    swapped = tensor_send(swapped, 0, 1)

    half = slabs.shape[0] // 2
    slabs_far = (x_send(slabs_left[:half], 1), x_send(slabs_right[half:], 3))
    quarters = (x + jnp.array([0, 3, 1, 2], jnp.int32)) % 4
    streams = [
        cotangent, before, after, hop_next, hop_prev, swapped, gathered, low, coef,
        slabs, slabs_left, slabs_right, *slabs_far,
    ]
    whole = lambda dims: pl.BlockSpec(dims, lambda i, *_: (0,) * len(dims))
    input_gradient = pl.pallas_call(
        frozen_kernel,
        grid_spec=pltpu.PrefetchScalarGridSpec(
            num_scalar_prefetch=2,
            grid=(1,),
            in_specs=[whole(v.shape) for v in streams],
            out_specs=whole((rows, window)),
            scratch_shapes=[pltpu.VMEM((rows, 16 * columns), BF)],
        ),
        out_shape=shape((rows, window), BF),
        compiler_params=pltpu.CompilerParams(vmem_limit_bytes=FULL_VMEM),
        cost_estimate=pl.CostEstimate(
            flops=2 * rows * window * 18 * columns, bytes_accessed=8 * 2**20, transcendentals=0
        ),
    )(slots, quarters, *streams)
    grad_a, grad_b = call(
        sum_kernel,
        [VMEM],
        [shape((owned, window), F32), shape((owned, columns), F32)],
        0,
        8,
    )(terms)
    return (input_gradient, grad_a, grad_b)


def solution(mesh):
    in_specs = (
        P("dp", "tensor"),
        P("dp", None, "tensor"),
        P(None, None, "tensor"),
        P("dp", "tensor"),
        P("dp", "tensor"),
        P(),
        P("dp"),
        P("dp"),
        P("dp"),
        P("dp"),
    )
    out_specs = (P("dp", "tensor"), P("dp", "tensor"), P("dp", "tensor"))
    return jax.shard_map(shards, mesh=mesh, in_specs=in_specs, out_specs=out_specs, check_vma=False)
```

```python
import functools

import jax
import jax.numpy as jnp
from jax import lax
from jax.experimental import pallas as pl
from jax.experimental.pallas import tpu as pltpu
from jax.sharding import PartitionSpec as P

BLOCK = 128
GSIZE = 8
SLOTS = 8
RANK = 64
LANES = 128
CHIPS = 4
FULL_VMEM = 60 * 2**20
LOWRANK_MULTIPLIER = 2.0
BF = jnp.bfloat16
F32 = jnp.float32
VMEM = pl.BlockSpec(memory_space=pltpu.VMEM)
SMEM = pl.BlockSpec(memory_space=pltpu.SMEM)


def dot(a, b, ca, cb):
    return lax.dot_general(a, b, (((ca,), (cb,)), ((), ())), preferred_element_type=F32)


def call(kernel, in_specs, shapes, flops, mib):
    single = not isinstance(shapes, (list, tuple))
    shapes = [shapes] if single else list(shapes)
    return pl.pallas_call(
        kernel,
        in_specs=in_specs,
        out_specs=VMEM if single else [VMEM] * len(shapes),
        out_shape=shapes[0] if single else shapes,
        compiler_params=pltpu.CompilerParams(vmem_limit_bytes=mib * 2**20),
        cost_estimate=pl.CostEstimate(flops=flops, bytes_accessed=2**20, transcendentals=0),
    )


def tensor_send(value, chip_step, core_flip):
    pairs = [
        (y * 2 + c, (y + chip_step) % CHIPS * 2 + (c ^ core_flip))
        for y in range(CHIPS)
        for c in range(2)
    ]
    return lax.ppermute(value, "tensor", pairs)


def x_send(value, step):
    pairs = [(i, i // 4 * 4 + (i + step) % 4) for i in range(lax.axis_size("dp"))]
    return lax.ppermute(value, "dp", pairs)


def pack_kernel(prompt, reward, down_ref, up_ref, out_ref):
    shape = (down_ref.shape[0], LANES)
    row = lax.broadcasted_iota(jnp.int32, shape, 0)
    lane = lax.broadcasted_iota(jnp.int32, shape, 1)
    blocks = reward.shape[1]
    rewards = jnp.zeros(shape, F32)
    prompts = jnp.full(shape, -1.0, F32)
    for b in range(blocks):
        one = (slice(0, 1), slice(b, b + 1))
        rewards = jnp.where(lane % blocks == b, reward[one], rewards)
        prompts = jnp.where(lane == b, prompt[one].astype(F32), prompts)
    high = rewards.astype(BF).astype(F32)
    rest = rewards - high
    middle = rest.astype(BF).astype(F32)
    part = lane // blocks
    parts = jnp.where(part == 0, high, jnp.where(part == 1, middle, rest - middle))
    parts = jnp.where(part < 3, parts, 0.0)
    facts = jnp.where(row == 0, parts, jnp.where(row == 1, prompts, 0.0)).astype(BF)
    packed = jnp.concatenate([down_ref[...], up_ref[...], facts], axis=1)
    for i in range(out_ref.shape[0]):
        out_ref[i] = packed


def streamed(kernel, blocks, out):
    whole = lambda shape: pl.BlockSpec(shape, lambda i: (0,) * len(shape))
    return pl.pallas_call(
        kernel,
        grid=(1,),
        in_specs=[whole(shape) for shape in blocks],
        out_specs=whole(out),
        out_shape=jax.ShapeDtypeStruct(out, BF),
        compiler_params=pltpu.CompilerParams(vmem_limit_bytes=FULL_VMEM),
    )


def assemble_kernel(cuts, *refs):
    *pieces, out_ref = refs
    at = 0
    for piece, (start, stop) in zip(pieces, cuts, strict=True):
        out_ref[at : at + stop - start] = piece[start:stop]
        at += stop - start


def assemble(*pieces):
    arrays = [p[0] for p in pieces]
    cuts = [p[1:] for p in pieces]
    columns = arrays[0].shape[1]
    total = sum(stop - start for start, stop in cuts)
    whole = lambda shape: pl.BlockSpec(shape, lambda i: (0,) * len(shape))
    return pl.pallas_call(
        functools.partial(assemble_kernel, cuts),
        grid=(1,),
        in_specs=[whole(v.shape) for v in arrays],
        out_specs=whole((total, columns)),
        out_shape=jax.ShapeDtypeStruct((total, columns), BF),
        compiler_params=pltpu.CompilerParams(vmem_limit_bytes=24 * 2**20),
    )(*arrays)


def payload_kernel(places, *refs):
    slabs, outs = refs[:8], refs[8:]
    tile = slabs[0].shape[1]
    for out_ref, units in zip(outs, ((0, 2), (1,), (3, 5), (4,), (6,), (7,)), strict=True):
        at = 0
        for i in units:
            for j in range(2):
                out_ref[at : at + tile] = slabs[i][j]
                at += tile


def payloads(places, weight, tile):
    columns = weight.shape[2]
    slab = [
        pl.BlockSpec((2, tile, columns), lambda g, p, i=i: (0, p[i], 0)) for i in range(8)
    ]
    sizes = [n * 2 * tile for n in (2, 1, 2, 1, 1, 1)]
    return pl.pallas_call(
        payload_kernel,
        grid_spec=pltpu.PrefetchScalarGridSpec(
            num_scalar_prefetch=1,
            grid=(1,),
            in_specs=slab,
            out_specs=[pl.BlockSpec((n, columns), lambda g, p: (0, 0)) for n in sizes],
        ),
        out_shape=[jax.ShapeDtypeStruct((n, columns), BF) for n in sizes],
        compiler_params=pltpu.CompilerParams(vmem_limit_bytes=FULL_VMEM),
    )(places, *[weight] * 8)


def factor_rows(ref, slot, start, size):
    owners = ref.shape[0] // SLOTS
    return ref[pl.ds(slot * owners, owners), :, pl.ds(start, size)].reshape(RANK, size)


def low_kernel(
    slots, live, prompt, reward, gathered_ref, x_ref, cot_ref, low_ref, weighted_ref, coef_ref
):
    window = x_ref.shape[1]
    columns = cot_ref.shape[2]
    blocks = reward.shape[0]
    facts = gathered_ref[:, :, window + columns :].astype(F32)
    row = lax.broadcasted_iota(jnp.int32, facts.shape, 1)
    parts = jnp.sum(jnp.where(row == 0, facts, 0.0), axis=1)
    prompts = jnp.sum(jnp.where(row == 1, facts, 0.0), axis=1)
    rewards = parts + pltpu.roll(parts, LANES - blocks, 1)
    rewards = rewards + pltpu.roll(parts, LANES - 2 * blocks, 1)
    place = lax.broadcasted_iota(jnp.int32, (BLOCK, 1), 0)
    whole = lambda v: jnp.sum(jnp.sum(v, axis=1, keepdims=True), axis=0, keepdims=True)
    for b in range(blocks):
        same = prompts == prompt[b].astype(F32)
        mean = whole(jnp.where(same, rewards, 0.0)) / GSIZE
        square = whole(jnp.where(same, rewards * rewards, 0.0)) / GSIZE
        spread = jnp.sqrt(jnp.maximum(square - mean * mean, 1.0))
        advantage = (reward[b] - mean) / spread
        coef = jnp.where(place < live[b], -advantage / GSIZE, 0.0)
        rows = pl.ds(b * BLOCK, BLOCK)
        weighted = (cot_ref[1, rows, :].astype(F32) * coef).astype(BF)
        low_h = dot(x_ref[rows, :], factor_rows(gathered_ref, slots[b], 0, window), 1, 1)
        low_g = dot(weighted, factor_rows(gathered_ref, slots[b], window, columns), 1, 1)
        low_ref[rows, :] = jnp.concatenate([low_h, low_g], axis=1)
        weighted_ref[rows, :] = weighted
        coef_ref[rows, :] = coef


def terms_kernel(slots, own, received, x_ref, weighted_ref, terms_ref, low_ref):
    window = x_ref.shape[1]
    columns = weighted_ref.shape[1]
    owners, owned = terms_ref.shape[0] // SLOTS, terms_ref.shape[1]
    low = own[...].astype(F32) + received[...].astype(F32)
    low_ref[...] = low.astype(BF)
    for i in range(terms_ref.shape[0]):
        terms_ref[i] = jnp.zeros(terms_ref.shape[1:], BF)
    for b in range(x_ref.shape[0] // BLOCK):
        rows = pl.ds(b * BLOCK, BLOCK)
        low = low_ref[rows, :]
        down = LOWRANK_MULTIPLIER * dot(low, x_ref[rows, :], 0, 0)[RANK:]
        up = LOWRANK_MULTIPLIER * dot(low, weighted_ref[rows, :], 0, 0)[:RANK]
        place = pl.ds(slots[b] * owners, owners)
        terms_ref[place, :, :window] = down.astype(BF).reshape(owners, owned, window)
        terms_ref[place, :, window:] = up.astype(BF).reshape(owners, owned, columns)


def quarter(weighted, parts, low_ref, gathered_ref, slots, start, tile):
    slabs = [p[i * tile : (i + 1) * tile] for p in parts for i in range(p.shape[0] // tile)]
    total = dot(weighted[...], jnp.concatenate(slabs, axis=1), 1, 1)
    extra = []
    for b in range(total.shape[0] // BLOCK):
        factor = factor_rows(gathered_ref, slots[b], start, tile)
        factor = jnp.concatenate([jnp.zeros_like(factor), factor], axis=0)
        low = low_ref[b * BLOCK : (b + 1) * BLOCK, :]
        extra.append(LOWRANK_MULTIPLIER * dot(low, factor, 1, 0))
    return (total + jnp.concatenate(extra, axis=0)).astype(BF)


def near_kernel(slots, quarters, cots, others, gathered_ref, low_ref, coef_ref, *refs):
    *slabs, out_ref, weighted = refs
    rows, columns = coef_ref.shape[0], cots.shape[1]
    tile = rows // 2
    coef = coef_ref[...]
    count = cots.shape[0] // rows
    for i in range(2 * count):
        piece = (cots, others)[i // count][i % count * rows : (i % count + 1) * rows]
        weighted[:, i * columns : (i + 1) * columns] = (piece.astype(F32) * coef).astype(BF)
    for r, part in enumerate(slabs):
        start = pl.multiple_of(quarters[r] * tile, tile)
        out_ref[:, pl.ds(start, tile)] = quarter(
            weighted, (part,), low_ref, gathered_ref, slots, start, tile
        )


def far_kernel(slots, quarters, near_ref, weighted, gathered_ref, low_ref, first, second, out_ref):
    tile = out_ref.shape[1]
    out_ref[...] = quarter(weighted, (first, second), low_ref, gathered_ref, slots, 0, tile)


def frozen_and_correction(slots, quarters, cots, adapter, near, far, window):
    gathered, low, coef = adapter
    rows, columns, tile = coef.shape[0], cots[0].shape[1], window // 4
    depth = 2 * cots[0].shape[0] // rows * columns
    shape = jax.ShapeDtypeStruct
    whole = lambda dims: pl.BlockSpec(dims, lambda i, *_: (0,) * len(dims))
    streams = [*cots, gathered, low, coef, *near]
    partial, weighted = pl.pallas_call(
        near_kernel,
        grid_spec=pltpu.PrefetchScalarGridSpec(
            num_scalar_prefetch=2,
            grid=(1,),
            in_specs=[whole(v.shape) for v in streams],
            out_specs=[whole((rows, window)), whole((rows, depth))],
        ),
        out_shape=[shape((rows, window), BF), shape((rows, depth), BF)],
        compiler_params=pltpu.CompilerParams(vmem_limit_bytes=FULL_VMEM),
    )(slots, quarters, *streams)
    owners, owned = gathered.shape[:2]
    return pl.pallas_call(
        far_kernel,
        grid_spec=pltpu.PrefetchScalarGridSpec(
            num_scalar_prefetch=2,
            grid=(1,),
            in_specs=[
                pl.BlockSpec(memory_space=pl.ANY),
                whole(weighted.shape),
                pl.BlockSpec((owners, owned, tile), lambda i, s, q: (0, 0, q[3])),
                whole(low.shape),
                *[whole(v.shape) for v in far],
            ],
            out_specs=pl.BlockSpec((rows, tile), lambda i, s, q: (0, q[3])),
        ),
        out_shape=shape((rows, window), BF),
        input_output_aliases={2: 0},
        compiler_params=pltpu.CompilerParams(vmem_limit_bytes=FULL_VMEM),
    )(slots, quarters, partial, weighted, gathered, low, *far)


def sum_kernel(terms_ref, down_ref, up_ref):
    window = down_ref.shape[1]
    total = terms_ref[0].astype(F32)
    for i in range(1, terms_ref.shape[0]):
        total = total + terms_ref[i].astype(F32)
    down_ref[...] = total[:, :window]
    up_ref[...] = total[:, window:]


def shards(
    normed_input_rows,
    key_value_cotangent,
    key_value_weight,
    adapter_down_factors,
    adapter_up_factors,
    slot_adapter,
    adapter_of_block,
    live_rows_of_block,
    prompt_of_block,
    reward_of_block,
):
    rows, window = normed_input_rows.shape
    columns = key_value_cotangent.shape[2]
    dp = lax.axis_size("dp")
    owned = adapter_down_factors.shape[0]
    te = lax.axis_index("tensor")
    chip, core = te // 2, te % 2
    x = lax.axis_index("dp") % 4
    tile = window // 4
    shape = jax.ShapeDtypeStruct
    slots = jnp.sum(
        jnp.where(
            adapter_of_block[:, None] == slot_adapter[None, :], jnp.arange(SLOTS, dtype=jnp.int32), 0
        ),
        axis=1,
    )

    packed = streamed(
        pack_kernel,
        [(1, 4), (1, 4), (owned, window), (owned, columns)],
        (dp, owned, window + columns + LANES),
    )(
        prompt_of_block.reshape(1, -1),
        reward_of_block.reshape(1, -1),
        adapter_down_factors,
        adapter_up_factors,
    )
    gathered = lax.all_to_all(packed, "dp", 0, 0)

    cotangent = jnp.transpose(key_value_cotangent, (1, 0, 2))
    steps = jnp.array([[1, 0], [1, 1], [2, 0], [3, 0], [3, 1], [2, 1], [0, 0], [0, 1]], jnp.int32)
    targets = (chip + steps[:, 0]) % CHIPS * 2 + (core + steps[:, 1]) % 2
    to_next, next_other, to_prev, prev_other, mine, other = payloads(
        targets * 4 + x, key_value_weight, tile
    )
    before, after = tensor_send(to_next, 1, 0), tensor_send(to_prev, 3, 0)
    before_other, after_other = tensor_send(next_other, 1, 1), tensor_send(prev_other, 3, 1)
    partner = tensor_send(other, 0, 1)
    unit = 2 * tile
    hop_next, hop_prev = lax.optimization_barrier((before[unit:], after[unit:]))
    hop_next, hop_prev = tensor_send(hop_next, 1, 0), tensor_send(hop_prev, 3, 1)
    pieces = mine, before, after, hop_next, partner, before_other, after_other, hop_prev
    slabs = assemble(*[(piece, 0, unit) for piece in pieces])
    flat = cotangent.reshape(2 * rows, columns)
    gathered, slabs, flat = lax.optimization_barrier((gathered, slabs, flat))

    low, weighted_value, coef = call(
        low_kernel,
        [SMEM] * 4 + [VMEM] * 3,
        [shape((rows, 2 * RANK), F32), shape((rows, columns), BF), shape((rows, 1), F32)],
        2 * rows * RANK * window,
        16,
    )(
        slots,
        live_rows_of_block,
        prompt_of_block,
        reward_of_block,
        gathered,
        normed_input_rows,
        cotangent,
    )
    low = (low + tensor_send(low, 0, 1)).astype(BF)
    for swap in (1, 3):
        pairs = [(y * 2 + c, (y ^ swap) * 2 + c) for y in range(CHIPS) for c in range(2)]
        sent = low
        received = lax.ppermute(sent, "tensor", pairs)
        if swap == 1:
            low = (sent.astype(F32) + received.astype(F32)).astype(BF)
    slabs_left, slabs_right = x_send(slabs, 1), x_send(slabs, 3)
    cot_before, cot_after = tensor_send(flat, 1, 0), tensor_send(flat, 3, 0)

    terms, low = call(
        terms_kernel,
        [SMEM] + [VMEM] * 4,
        [shape((dp, owned, window + columns), BF), shape((rows, 2 * RANK), BF)],
        4 * rows * RANK * window,
        16,
    )(slots, sent, received, normed_input_rows, weighted_value)
    cot_next = tensor_send(cot_before[:rows], 1, 0)
    cot_prev = tensor_send(cot_after[rows:], 3, 0)
    cots = assemble(
        (flat, 0, 2 * rows),
        (cot_before, 0, 2 * rows),
        (cot_after, 0, 2 * rows),
        (cot_next, 0, rows),
        (cot_prev, 0, rows),
    )
    cots_other = tensor_send(cots, 0, 1)
    terms, slabs_left, slabs_right, cots, cots_other = lax.optimization_barrier(
        (terms, slabs_left, slabs_right, cots, cots_other)
    )
    terms = lax.all_to_all(terms, "dp", 0, 0)
    half = slabs.shape[0] // 2
    slabs_far = (x_send(slabs_left[:half], 1), x_send(slabs_right[half:], 3))
    quarters = (x + jnp.array([0, 3, 1, 2], jnp.int32)) % 4
    input_gradient = frozen_and_correction(
        slots,
        quarters,
        (cots, cots_other),
        (gathered, low, coef),
        (slabs, slabs_left, slabs_right),
        slabs_far,
        window,
    )
    grad_a, grad_b = call(
        sum_kernel,
        [VMEM],
        [shape((owned, window), F32), shape((owned, columns), F32)],
        0,
        8,
    )(terms)
    return (input_gradient, grad_a, grad_b)


def solution(mesh):
    in_specs = (
        P("dp", "tensor"),
        P("dp", None, "tensor"),
        P(None, None, "tensor"),
        P("dp", "tensor"),
        P("dp", "tensor"),
        P(),
        P("dp"),
        P("dp"),
        P("dp"),
        P("dp"),
    )
    out_specs = (P("dp", "tensor"), P("dp", "tensor"), P("dp", "tensor"))
    return jax.shard_map(shards, mesh=mesh, in_specs=in_specs, out_specs=out_specs, check_vma=False)
```

```python
import functools

import jax
import jax.numpy as jnp
from jax import lax
from jax.experimental import pallas as pl
from jax.experimental.pallas import tpu as pltpu
from jax.sharding import PartitionSpec as P

BLOCK = 128
GSIZE = 8
SLOTS = 8
RANK = 64
LANES = 128
CHIPS = 4
FULL_VMEM = 60 * 2**20
LOWRANK_MULTIPLIER = 2.0
BF = jnp.bfloat16
F32 = jnp.float32
VMEM = pl.BlockSpec(memory_space=pltpu.VMEM)
SMEM = pl.BlockSpec(memory_space=pltpu.SMEM)


def dot(a, b, ca, cb):
    return lax.dot_general(a, b, (((ca,), (cb,)), ((), ())), preferred_element_type=F32)


def call(kernel, in_specs, shapes, flops, mib):
    single = not isinstance(shapes, (list, tuple))
    shapes = [shapes] if single else list(shapes)
    return pl.pallas_call(
        kernel,
        in_specs=in_specs,
        out_specs=VMEM if single else [VMEM] * len(shapes),
        out_shape=shapes[0] if single else shapes,
        compiler_params=pltpu.CompilerParams(vmem_limit_bytes=mib * 2**20),
        cost_estimate=pl.CostEstimate(flops=flops, bytes_accessed=2**20, transcendentals=0),
    )


def tensor_send(value, chip_step, core_flip):
    pairs = [
        (y * 2 + c, (y + chip_step) % CHIPS * 2 + (c ^ core_flip))
        for y in range(CHIPS)
        for c in range(2)
    ]
    return lax.ppermute(value, "tensor", pairs)


def x_send(value, step):
    pairs = [(i, i // 4 * 4 + (i + step) % 4) for i in range(lax.axis_size("dp"))]
    return lax.ppermute(value, "dp", pairs)


def pack_kernel(prompt, reward, down_ref, up_ref, out_ref):
    shape = (down_ref.shape[0], LANES)
    row = lax.broadcasted_iota(jnp.int32, shape, 0)
    lane = lax.broadcasted_iota(jnp.int32, shape, 1)
    blocks = reward.shape[1]
    rewards = jnp.zeros(shape, F32)
    prompts = jnp.full(shape, -1.0, F32)
    for b in range(blocks):
        one = (slice(0, 1), slice(b, b + 1))
        rewards = jnp.where(lane % blocks == b, reward[one], rewards)
        prompts = jnp.where(lane == b, prompt[one].astype(F32), prompts)
    high = rewards.astype(BF).astype(F32)
    rest = rewards - high
    middle = rest.astype(BF).astype(F32)
    part = lane // blocks
    parts = jnp.where(part == 0, high, jnp.where(part == 1, middle, rest - middle))
    parts = jnp.where(part < 3, parts, 0.0)
    facts = jnp.where(row == 0, parts, jnp.where(row == 1, prompts, 0.0)).astype(BF)
    packed = jnp.concatenate([down_ref[...], up_ref[...], facts], axis=1)
    for i in range(out_ref.shape[0]):
        out_ref[i] = packed


def streamed(kernel, blocks, out):
    whole = lambda shape: pl.BlockSpec(shape, lambda i: (0,) * len(shape))
    return pl.pallas_call(
        kernel,
        grid=(1,),
        in_specs=[whole(shape) for shape in blocks],
        out_specs=whole(out),
        out_shape=jax.ShapeDtypeStruct(out, BF),
        compiler_params=pltpu.CompilerParams(vmem_limit_bytes=FULL_VMEM),
    )


def assemble_kernel(cuts, *refs):
    *pieces, out_ref = refs
    at = 0
    for piece, (start, stop) in zip(pieces, cuts, strict=True):
        out_ref[at : at + stop - start] = piece[start:stop]
        at += stop - start


def assemble(*pieces):
    arrays = [p[0] for p in pieces]
    cuts = [p[1:] for p in pieces]
    columns = arrays[0].shape[1]
    total = sum(stop - start for start, stop in cuts)
    whole = lambda shape: pl.BlockSpec(shape, lambda i: (0,) * len(shape))
    return pl.pallas_call(
        functools.partial(assemble_kernel, cuts),
        grid=(1,),
        in_specs=[whole(v.shape) for v in arrays],
        out_specs=whole((total, columns)),
        out_shape=jax.ShapeDtypeStruct((total, columns), BF),
        compiler_params=pltpu.CompilerParams(vmem_limit_bytes=24 * 2**20),
    )(*arrays)


def payload_kernel(places, *refs):
    slabs, outs = refs[:8], refs[8:]
    tile = slabs[0].shape[1]
    for out_ref, units in zip(outs, ((0, 2), (1,), (3, 5), (4,), (6,), (7,)), strict=True):
        at = 0
        for i in units:
            for j in range(2):
                out_ref[at : at + tile] = slabs[i][j]
                at += tile


def payloads(places, weight, tile):
    columns = weight.shape[2]
    slab = [
        pl.BlockSpec((2, tile, columns), lambda g, p, i=i: (0, p[i], 0)) for i in range(8)
    ]
    sizes = [n * 2 * tile for n in (2, 1, 2, 1, 1, 1)]
    return pl.pallas_call(
        payload_kernel,
        grid_spec=pltpu.PrefetchScalarGridSpec(
            num_scalar_prefetch=1,
            grid=(1,),
            in_specs=slab,
            out_specs=[pl.BlockSpec((n, columns), lambda g, p: (0, 0)) for n in sizes],
        ),
        out_shape=[jax.ShapeDtypeStruct((n, columns), BF) for n in sizes],
        compiler_params=pltpu.CompilerParams(vmem_limit_bytes=FULL_VMEM),
    )(places, *[weight] * 8)


def factor_rows(table_ref, slot, start, size):
    return table_ref[pl.ds(pl.multiple_of(slot * RANK, RANK), RANK), pl.ds(start, size)]


def low_kernel(
    slots, live, prompt, reward, own, before, after, far_first, far_second, x_ref, cot_ref, *outs
):
    low_ref, weighted_ref, coef_ref, table_ref = outs
    window = x_ref.shape[1]
    columns = cot_ref.shape[2]
    blocks = reward.shape[0]
    owned, half = own.shape[1], far_first.shape[0]
    for k in range(SLOTS):
        far = far_first[k] if k < half else far_second[k - half]
        for i, piece in enumerate((own[k], before[k], after[k], far)):
            table_ref[k * RANK + i * owned : k * RANK + (i + 1) * owned] = piece
    facts = table_ref[:, window + columns :].astype(F32).reshape(-1, owned, LANES)
    row = lax.broadcasted_iota(jnp.int32, facts.shape, 1)
    parts = jnp.sum(jnp.where(row == 0, facts, 0.0), axis=1)
    prompts = jnp.sum(jnp.where(row == 1, facts, 0.0), axis=1)
    rewards = parts + pltpu.roll(parts, LANES - blocks, 1)
    rewards = rewards + pltpu.roll(parts, LANES - 2 * blocks, 1)
    place = lax.broadcasted_iota(jnp.int32, (BLOCK, 1), 0)
    whole = lambda v: jnp.sum(jnp.sum(v, axis=1, keepdims=True), axis=0, keepdims=True)
    for b in range(blocks):
        same = prompts == prompt[b].astype(F32)
        mean = whole(jnp.where(same, rewards, 0.0)) / GSIZE
        square = whole(jnp.where(same, rewards * rewards, 0.0)) / GSIZE
        spread = jnp.sqrt(jnp.maximum(square - mean * mean, 1.0))
        advantage = (reward[b] - mean) / spread
        coef = jnp.where(place < live[b], -advantage / GSIZE, 0.0)
        rows = pl.ds(b * BLOCK, BLOCK)
        weighted = (cot_ref[1, rows, :].astype(F32) * coef).astype(BF)
        low_h = dot(x_ref[rows, :], factor_rows(table_ref, slots[b], 0, window), 1, 1)
        low_g = dot(weighted, factor_rows(table_ref, slots[b], window, columns), 1, 1)
        low_ref[rows, :] = jnp.concatenate([low_h, low_g], axis=1)
        weighted_ref[rows, :] = weighted
        coef_ref[rows, :] = coef


def terms_kernel(
    slots, order, own, first, second, third, x_ref, weighted_ref, terms_ref, low_ref
):
    window = x_ref.shape[1]
    owned, owners = terms_ref.shape[1], terms_ref.shape[0] // SLOTS
    low = own[...].astype(F32) + first[...].astype(F32)
    low = (low + second[...].astype(F32)) + third[...].astype(F32)
    low_ref[...] = low.astype(BF)
    for i in range(terms_ref.shape[0]):
        terms_ref[i] = jnp.zeros(terms_ref.shape[1:], BF)
    for b in range(x_ref.shape[0] // BLOCK):
        rows = pl.ds(b * BLOCK, BLOCK)
        low = low_ref[rows, :]
        down = LOWRANK_MULTIPLIER * dot(low, x_ref[rows, :], 0, 0)[RANK:]
        up = LOWRANK_MULTIPLIER * dot(low, weighted_ref[rows, :], 0, 0)[:RANK]
        for i in range(owners):
            place = slots[b] * owners + order[i]
            cut = slice(i * owned, (i + 1) * owned)
            terms_ref[place, :, :window] = down[cut].astype(BF)
            terms_ref[place, :, window:] = up[cut].astype(BF)


def quarter(weighted, parts, low_ref, table_ref, slots, start, tile):
    slabs = [p[i * tile : (i + 1) * tile] for p in parts for i in range(p.shape[0] // tile)]
    total = dot(weighted[...], jnp.concatenate(slabs, axis=1), 1, 1)
    extra = []
    for b in range(total.shape[0] // BLOCK):
        factor = factor_rows(table_ref, slots[b], start, tile)
        factor = jnp.concatenate([jnp.zeros_like(factor), factor], axis=0)
        low = low_ref[b * BLOCK : (b + 1) * BLOCK, :]
        extra.append(LOWRANK_MULTIPLIER * dot(low, factor, 1, 0))
    return (total + jnp.concatenate(extra, axis=0)).astype(BF)


def near_kernel(slots, quarters, cots, others, table_ref, low_ref, coef_ref, *refs):
    *slabs, out_ref, weighted = refs
    rows, columns = coef_ref.shape[0], cots.shape[1]
    tile = rows // 2
    coef = coef_ref[...]
    count = cots.shape[0] // rows
    for i in range(2 * count):
        piece = (cots, others)[i // count][i % count * rows : (i % count + 1) * rows]
        weighted[:, i * columns : (i + 1) * columns] = (piece.astype(F32) * coef).astype(BF)
    for r, part in enumerate(slabs):
        start = pl.multiple_of(quarters[r] * tile, tile)
        out_ref[:, pl.ds(start, tile)] = quarter(
            weighted, (part,), low_ref, table_ref, slots, start, tile
        )


def far_kernel(slots, quarters, near_ref, weighted, table_ref, low_ref, first, second, out_ref):
    tile = out_ref.shape[1]
    out_ref[...] = quarter(weighted, (first, second), low_ref, table_ref, slots, 0, tile)


def frozen_and_correction(slots, quarters, cots, adapter, near, far, window):
    table, low, coef = adapter
    rows, columns, tile = coef.shape[0], cots[0].shape[1], window // 4
    depth = 2 * cots[0].shape[0] // rows * columns
    shape = jax.ShapeDtypeStruct
    whole = lambda dims: pl.BlockSpec(dims, lambda i, *_: (0,) * len(dims))
    streams = [*cots, table, low, coef, *near]
    partial, weighted = pl.pallas_call(
        near_kernel,
        grid_spec=pltpu.PrefetchScalarGridSpec(
            num_scalar_prefetch=2,
            grid=(1,),
            in_specs=[whole(v.shape) for v in streams],
            out_specs=[whole((rows, window)), whole((rows, depth))],
        ),
        out_shape=[shape((rows, window), BF), shape((rows, depth), BF)],
        compiler_params=pltpu.CompilerParams(vmem_limit_bytes=FULL_VMEM),
    )(slots, quarters, *streams)
    return pl.pallas_call(
        far_kernel,
        grid_spec=pltpu.PrefetchScalarGridSpec(
            num_scalar_prefetch=2,
            grid=(1,),
            in_specs=[
                pl.BlockSpec(memory_space=pl.ANY),
                whole(weighted.shape),
                pl.BlockSpec((table.shape[0], tile), lambda i, s, q: (0, q[3])),
                whole(low.shape),
                *[whole(v.shape) for v in far],
            ],
            out_specs=pl.BlockSpec((rows, tile), lambda i, s, q: (0, q[3])),
        ),
        out_shape=shape((rows, window), BF),
        input_output_aliases={2: 0},
        compiler_params=pltpu.CompilerParams(vmem_limit_bytes=FULL_VMEM),
    )(slots, quarters, partial, weighted, table, low, *far)


def sum_kernel(terms_ref, down_ref, up_ref):
    window = down_ref.shape[1]
    total = terms_ref[0].astype(F32)
    for i in range(1, terms_ref.shape[0]):
        total = total + terms_ref[i].astype(F32)
    down_ref[...] = total[:, :window]
    up_ref[...] = total[:, window:]


def shards(
    normed_input_rows,
    key_value_cotangent,
    key_value_weight,
    adapter_down_factors,
    adapter_up_factors,
    slot_adapter,
    adapter_of_block,
    live_rows_of_block,
    prompt_of_block,
    reward_of_block,
):
    rows, window = normed_input_rows.shape
    columns = key_value_cotangent.shape[2]
    dp = lax.axis_size("dp")
    owned = adapter_down_factors.shape[0]
    te = lax.axis_index("tensor")
    chip, core = te // 2, te % 2
    x = lax.axis_index("dp") % 4
    tile = window // 4
    shape = jax.ShapeDtypeStruct
    slots = jnp.sum(
        jnp.where(
            adapter_of_block[:, None] == slot_adapter[None, :], jnp.arange(SLOTS, dtype=jnp.int32), 0
        ),
        axis=1,
    )

    packed = streamed(
        pack_kernel,
        [(1, 4), (1, 4), (owned, window), (owned, columns)],
        (dp // 4, owned, window + columns + LANES),
    )(
        prompt_of_block.reshape(1, -1),
        reward_of_block.reshape(1, -1),
        adapter_down_factors,
        adapter_up_factors,
    )
    along_z = [[z * 4 + i for z in range(dp // 4)] for i in range(4)]
    own_x = lax.all_to_all(packed, "dp", 0, 0, axis_index_groups=along_z)

    cotangent = jnp.transpose(key_value_cotangent, (1, 0, 2))
    steps = jnp.array([[1, 0], [1, 1], [2, 0], [3, 0], [3, 1], [2, 1], [0, 0], [0, 1]], jnp.int32)
    targets = (chip + steps[:, 0]) % CHIPS * 2 + (core + steps[:, 1]) % 2
    to_next, next_other, to_prev, prev_other, mine, other = payloads(
        targets * 4 + x, key_value_weight, tile
    )
    unit = 2 * tile
    chain = (
        tensor_send(to_next, 1, 0),
        tensor_send(to_prev, 3, 0),
        tensor_send(next_other, 1, 1),
        tensor_send(prev_other, 3, 1),
        tensor_send(other, 0, 1),
    )
    own_x, chain = lax.optimization_barrier((own_x, chain))
    before, after, before_other, after_other, partner = chain
    before_x, after_x = x_send(own_x, 1), x_send(own_x, 3)
    hop_next = tensor_send(before[unit:], 1, 0)
    hop_prev = tensor_send(after[unit:], 3, 1)
    split = dp // 8
    far_x = x_send(before_x[:split], 1), x_send(after_x[split:], 3)
    gathered = own_x, before_x, after_x, *far_x
    gathered, hop_next, hop_prev = lax.optimization_barrier((gathered, hop_next, hop_prev))
    flat = cotangent.reshape(2 * rows, columns)
    slabs = assemble(
        *[(piece, 0, unit) for piece in (mine, before, after, hop_next)],
        *[(piece, 0, unit) for piece in (partner, before_other, after_other)],
        (hop_prev, 0, unit),
    )
    quarters = (x + jnp.array([0, 3, 1, 2], jnp.int32)) % 4

    low, weighted_value, coef, table = call(
        low_kernel,
        [SMEM] * 4 + [VMEM] * 7,
        [
            shape((rows, 2 * RANK), F32),
            shape((rows, columns), BF),
            shape((rows, 1), F32),
            shape((SLOTS * RANK, window + columns + LANES), BF),
        ],
        2 * rows * RANK * window,
        16,
    )(
        slots,
        live_rows_of_block,
        prompt_of_block,
        reward_of_block,
        *gathered,
        normed_input_rows,
        cotangent,
    )
    low = (low + tensor_send(low, 0, 1)).astype(BF)
    lows = [low] + [tensor_send(low, s, 0) for s in (1, 3, 2)]
    slabs_left, slabs_right = x_send(slabs, 1), x_send(slabs, 3)

    terms, low = call(
        terms_kernel,
        [SMEM] * 2 + [VMEM] * 6,
        [shape((dp, owned, window + columns), BF), shape((rows, 2 * RANK), BF)],
        4 * rows * RANK * window,
        16,
    )(slots, quarters, *lows, normed_input_rows, weighted_value)
    terms, slabs_left, slabs_right = lax.optimization_barrier((terms, slabs_left, slabs_right))
    terms = lax.all_to_all(terms, "dp", 0, 0)
    half = slabs.shape[0] // 2
    slabs_far = (x_send(slabs_left[:half], 1), x_send(slabs_right[half:], 3))
    cot_before, cot_after = tensor_send(flat, 1, 0), tensor_send(flat, 3, 0)
    cot_next = tensor_send(cot_before[:rows], 1, 0)
    cot_prev = tensor_send(cot_after[rows:], 3, 0)
    cots = assemble(
        (flat, 0, 2 * rows),
        (cot_before, 0, 2 * rows),
        (cot_after, 0, 2 * rows),
        (cot_next, 0, rows),
        (cot_prev, 0, rows),
    )
    cots_other = tensor_send(cots, 0, 1)
    input_gradient = frozen_and_correction(
        slots,
        quarters,
        (cots, cots_other),
        (table, low, coef),
        (slabs, slabs_left, slabs_right),
        slabs_far,
        window,
    )
    grad_a, grad_b = call(
        sum_kernel,
        [VMEM],
        [shape((owned, window), F32), shape((owned, columns), F32)],
        0,
        8,
    )(terms)
    return (input_gradient, grad_a, grad_b)


def solution(mesh):
    in_specs = (
        P("dp", "tensor"),
        P("dp", None, "tensor"),
        P(None, None, "tensor"),
        P("dp", "tensor"),
        P("dp", "tensor"),
        P(),
        P("dp"),
        P("dp"),
        P("dp"),
        P("dp"),
    )
    out_specs = (P("dp", "tensor"), P("dp", "tensor"), P("dp", "tensor"))
    return jax.shard_map(shards, mesh=mesh, in_specs=in_specs, out_specs=out_specs, check_vma=False)
```

```python
import functools

import jax
import jax.numpy as jnp
from jax import lax
from jax.experimental import pallas as pl
from jax.experimental.pallas import tpu as pltpu
from jax.sharding import PartitionSpec as P

BLOCK = 128
GSIZE = 8
SLOTS = 8
RANK = 64
LANES = 128
CHIPS = 4
FULL_VMEM = 60 * 2**20
LOWRANK_MULTIPLIER = 2.0
BF = jnp.bfloat16
F32 = jnp.float32
VMEM = pl.BlockSpec(memory_space=pltpu.VMEM)
SMEM = pl.BlockSpec(memory_space=pltpu.SMEM)


def dot(a, b, ca, cb):
    return lax.dot_general(a, b, (((ca,), (cb,)), ((), ())), preferred_element_type=F32)


def call(kernel, in_specs, shapes, flops, mib):
    single = not isinstance(shapes, (list, tuple))
    shapes = [shapes] if single else list(shapes)
    return pl.pallas_call(
        kernel,
        in_specs=in_specs,
        out_specs=VMEM if single else [VMEM] * len(shapes),
        out_shape=shapes[0] if single else shapes,
        compiler_params=pltpu.CompilerParams(vmem_limit_bytes=mib * 2**20),
        cost_estimate=pl.CostEstimate(flops=flops, bytes_accessed=2**20, transcendentals=0),
    )


def tensor_send(value, chip_step, core_flip):
    pairs = [
        (y * 2 + c, (y + chip_step) % CHIPS * 2 + (c ^ core_flip))
        for y in range(CHIPS)
        for c in range(2)
    ]
    return lax.ppermute(value, "tensor", pairs)


def x_send(value, step):
    pairs = [(i, i // 4 * 4 + (i + step) % 4) for i in range(lax.axis_size("dp"))]
    return lax.ppermute(value, "dp", pairs)


def pack_kernel(prompt, reward, down_ref, up_ref, out_ref):
    shape = (down_ref.shape[0], LANES)
    row = lax.broadcasted_iota(jnp.int32, shape, 0)
    lane = lax.broadcasted_iota(jnp.int32, shape, 1)
    blocks = reward.shape[1]
    rewards = jnp.zeros(shape, F32)
    prompts = jnp.full(shape, -1.0, F32)
    for b in range(blocks):
        one = (slice(0, 1), slice(b, b + 1))
        rewards = jnp.where(lane % blocks == b, reward[one], rewards)
        prompts = jnp.where(lane == b, prompt[one].astype(F32), prompts)
    high = rewards.astype(BF).astype(F32)
    rest = rewards - high
    middle = rest.astype(BF).astype(F32)
    part = lane // blocks
    parts = jnp.where(part == 0, high, jnp.where(part == 1, middle, rest - middle))
    parts = jnp.where(part < 3, parts, 0.0)
    facts = jnp.where(row == 0, parts, jnp.where(row == 1, prompts, 0.0)).astype(BF)
    packed = jnp.concatenate([down_ref[...], up_ref[...], facts], axis=1)
    for i in range(out_ref.shape[0]):
        out_ref[i] = packed


def streamed(kernel, blocks, out):
    whole = lambda shape: pl.BlockSpec(shape, lambda i: (0,) * len(shape))
    return pl.pallas_call(
        kernel,
        grid=(1,),
        in_specs=[whole(shape) for shape in blocks],
        out_specs=whole(out),
        out_shape=jax.ShapeDtypeStruct(out, BF),
        compiler_params=pltpu.CompilerParams(vmem_limit_bytes=FULL_VMEM),
    )


def assemble_kernel(cuts, *refs):
    *pieces, out_ref = refs
    at = 0
    for piece, (start, stop) in zip(pieces, cuts, strict=True):
        out_ref[at : at + stop - start] = piece[start:stop]
        at += stop - start


def assemble(*pieces):
    arrays = [p[0] for p in pieces]
    cuts = [p[1:] for p in pieces]
    columns = arrays[0].shape[1]
    total = sum(stop - start for start, stop in cuts)
    whole = lambda shape: pl.BlockSpec(shape, lambda i: (0,) * len(shape))
    return pl.pallas_call(
        functools.partial(assemble_kernel, cuts),
        grid=(1,),
        in_specs=[whole(v.shape) for v in arrays],
        out_specs=whole((total, columns)),
        out_shape=jax.ShapeDtypeStruct((total, columns), BF),
        compiler_params=pltpu.CompilerParams(vmem_limit_bytes=24 * 2**20),
    )(*arrays)


def payload_kernel(places, *refs):
    *slabs, cot_ref, next_ref, next_other, prev_ref, prev_other, mine_ref, other_ref = refs
    tile, rows = slabs[0].shape[1], cot_ref.shape[1]
    key, value = (cot_ref.at[0],), (cot_ref.at[1],)
    slab = lambda i: (slabs[i].at[0], slabs[i].at[1])
    orders = (
        (next_ref, (slab(0), slab(2), key, value)),
        (next_other, (slab(1),)),
        (prev_ref, (slab(3), key, value, slab(5))),
        (prev_other, (slab(4),)),
        (mine_ref, (slab(6),)),
        (other_ref, (slab(7),)),
    )
    for out_ref, units in orders:
        at = 0
        for piece in (p for unit in units for p in unit):
            out_ref[at : at + piece.shape[0]] = piece[...]
            at += piece.shape[0]


def payloads(places, weight, cotangent, tile):
    columns = weight.shape[2]
    slab = [
        pl.BlockSpec((2, tile, columns), lambda g, p, i=i: (0, p[i], 0)) for i in range(8)
    ]
    sizes = [n * 2 * tile for n in (4, 1, 4, 1, 1, 1)]
    return pl.pallas_call(
        payload_kernel,
        grid_spec=pltpu.PrefetchScalarGridSpec(
            num_scalar_prefetch=1,
            grid=(1,),
            in_specs=[*slab, pl.BlockSpec(cotangent.shape, lambda g, p: (0, 0, 0))],
            out_specs=[pl.BlockSpec((n, columns), lambda g, p: (0, 0)) for n in sizes],
        ),
        out_shape=[jax.ShapeDtypeStruct((n, columns), BF) for n in sizes],
        compiler_params=pltpu.CompilerParams(vmem_limit_bytes=FULL_VMEM),
    )(places, *[weight] * 8, cotangent)


def factor_rows(ref, slot, start, size):
    owners = ref.shape[0] // SLOTS
    return ref[pl.ds(slot * owners, owners), :, pl.ds(start, size)].reshape(RANK, size)


def low_kernel(
    slots, live, prompt, reward, gathered_ref, x_ref, cot_ref, low_ref, weighted_ref, coef_ref
):
    window = x_ref.shape[1]
    columns = cot_ref.shape[2]
    blocks = reward.shape[0]
    facts = gathered_ref[:, :, window + columns :].astype(F32)
    row = lax.broadcasted_iota(jnp.int32, facts.shape, 1)
    parts = jnp.sum(jnp.where(row == 0, facts, 0.0), axis=1)
    prompts = jnp.sum(jnp.where(row == 1, facts, 0.0), axis=1)
    rewards = parts + pltpu.roll(parts, LANES - blocks, 1)
    rewards = rewards + pltpu.roll(parts, LANES - 2 * blocks, 1)
    place = lax.broadcasted_iota(jnp.int32, (BLOCK, 1), 0)
    whole = lambda v: jnp.sum(jnp.sum(v, axis=1, keepdims=True), axis=0, keepdims=True)
    for b in range(blocks):
        same = prompts == prompt[b].astype(F32)
        mean = whole(jnp.where(same, rewards, 0.0)) / GSIZE
        square = whole(jnp.where(same, rewards * rewards, 0.0)) / GSIZE
        spread = jnp.sqrt(jnp.maximum(square - mean * mean, 1.0))
        advantage = (reward[b] - mean) / spread
        coef = jnp.where(place < live[b], -advantage / GSIZE, 0.0)
        rows = pl.ds(b * BLOCK, BLOCK)
        weighted = (cot_ref[1, rows, :].astype(F32) * coef).astype(BF)
        low_h = dot(x_ref[rows, :], factor_rows(gathered_ref, slots[b], 0, window), 1, 1)
        low_g = dot(weighted, factor_rows(gathered_ref, slots[b], window, columns), 1, 1)
        low_ref[rows, :] = jnp.concatenate([low_h, low_g], axis=1)
        weighted_ref[rows, :] = weighted
        coef_ref[rows, :] = coef


def terms_kernel(slots, own, first, second, third, x_ref, weighted_ref, terms_ref, low_ref):
    window = x_ref.shape[1]
    columns = weighted_ref.shape[1]
    owners, owned = terms_ref.shape[0] // SLOTS, terms_ref.shape[1]
    low = own[...].astype(F32) + first[...].astype(F32)
    low = (low + second[...].astype(F32)) + third[...].astype(F32)
    low_ref[...] = low.astype(BF)
    for i in range(terms_ref.shape[0]):
        terms_ref[i] = jnp.zeros(terms_ref.shape[1:], BF)
    for b in range(x_ref.shape[0] // BLOCK):
        rows = pl.ds(b * BLOCK, BLOCK)
        low = low_ref[rows, :]
        down = LOWRANK_MULTIPLIER * dot(low, x_ref[rows, :], 0, 0)[RANK:]
        up = LOWRANK_MULTIPLIER * dot(low, weighted_ref[rows, :], 0, 0)[:RANK]
        place = pl.ds(slots[b] * owners, owners)
        terms_ref[place, :, :window] = down.astype(BF).reshape(owners, owned, window)
        terms_ref[place, :, window:] = up.astype(BF).reshape(owners, owned, columns)


def quarter(weighted, parts, low_ref, gathered_ref, slots, start, tile):
    slabs = [p[i * tile : (i + 1) * tile] for p in parts for i in range(p.shape[0] // tile)]
    total = dot(weighted[...], jnp.concatenate(slabs, axis=1), 1, 1)
    extra = []
    for b in range(total.shape[0] // BLOCK):
        factor = factor_rows(gathered_ref, slots[b], start, tile)
        factor = jnp.concatenate([jnp.zeros_like(factor), factor], axis=0)
        low = low_ref[b * BLOCK : (b + 1) * BLOCK, :]
        extra.append(LOWRANK_MULTIPLIER * dot(low, factor, 1, 0))
    return (total + jnp.concatenate(extra, axis=0)).astype(BF)


def near_kernel(slots, quarters, cots, others, gathered_ref, low_ref, coef_ref, *refs):
    *slabs, out_ref, weighted = refs
    rows, columns = coef_ref.shape[0], cots.shape[1]
    tile = rows // 2
    coef = coef_ref[...]
    count = cots.shape[0] // rows
    for i in range(2 * count):
        source = (cots, others)[(i // count + (i % count == count - 1)) % 2]
        piece = source[i % count * rows : (i % count + 1) * rows]
        weighted[:, i * columns : (i + 1) * columns] = (piece.astype(F32) * coef).astype(BF)
    for r, part in enumerate(slabs):
        start = pl.multiple_of(quarters[r] * tile, tile)
        out_ref[:, pl.ds(start, tile)] = quarter(
            weighted, (part,), low_ref, gathered_ref, slots, start, tile
        )


def far_kernel(slots, quarters, near_ref, weighted, gathered_ref, low_ref, first, second, out_ref):
    tile = out_ref.shape[1]
    out_ref[...] = quarter(weighted, (first, second), low_ref, gathered_ref, slots, 0, tile)


def frozen_and_correction(slots, quarters, cots, adapter, near, far, window):
    gathered, low, coef = adapter
    rows, columns, tile = coef.shape[0], cots[0].shape[1], window // 4
    depth = 2 * cots[0].shape[0] // rows * columns
    shape = jax.ShapeDtypeStruct
    whole = lambda dims: pl.BlockSpec(dims, lambda i, *_: (0,) * len(dims))
    streams = [*cots, gathered, low, coef, *near]
    partial, weighted = pl.pallas_call(
        near_kernel,
        grid_spec=pltpu.PrefetchScalarGridSpec(
            num_scalar_prefetch=2,
            grid=(1,),
            in_specs=[whole(v.shape) for v in streams],
            out_specs=[whole((rows, window)), whole((rows, depth))],
        ),
        out_shape=[shape((rows, window), BF), shape((rows, depth), BF)],
        compiler_params=pltpu.CompilerParams(vmem_limit_bytes=FULL_VMEM),
    )(slots, quarters, *streams)
    owners, owned = gathered.shape[:2]
    return pl.pallas_call(
        far_kernel,
        grid_spec=pltpu.PrefetchScalarGridSpec(
            num_scalar_prefetch=2,
            grid=(1,),
            in_specs=[
                pl.BlockSpec(memory_space=pl.ANY),
                whole(weighted.shape),
                pl.BlockSpec((owners, owned, tile), lambda i, s, q: (0, 0, q[3])),
                whole(low.shape),
                *[whole(v.shape) for v in far],
            ],
            out_specs=pl.BlockSpec((rows, tile), lambda i, s, q: (0, q[3])),
        ),
        out_shape=shape((rows, window), BF),
        input_output_aliases={2: 0},
        compiler_params=pltpu.CompilerParams(vmem_limit_bytes=FULL_VMEM),
    )(slots, quarters, partial, weighted, gathered, low, *far)


def sum_kernel(terms_ref, down_ref, up_ref):
    window = down_ref.shape[1]
    total = terms_ref[0].astype(F32)
    for i in range(1, terms_ref.shape[0]):
        total = total + terms_ref[i].astype(F32)
    down_ref[...] = total[:, :window]
    up_ref[...] = total[:, window:]


def shards(
    normed_input_rows,
    key_value_cotangent,
    key_value_weight,
    adapter_down_factors,
    adapter_up_factors,
    slot_adapter,
    adapter_of_block,
    live_rows_of_block,
    prompt_of_block,
    reward_of_block,
):
    rows, window = normed_input_rows.shape
    columns = key_value_cotangent.shape[2]
    dp = lax.axis_size("dp")
    owned = adapter_down_factors.shape[0]
    te = lax.axis_index("tensor")
    chip, core = te // 2, te % 2
    x = lax.axis_index("dp") % 4
    tile = window // 4
    shape = jax.ShapeDtypeStruct
    slots = jnp.sum(
        jnp.where(
            adapter_of_block[:, None] == slot_adapter[None, :], jnp.arange(SLOTS, dtype=jnp.int32), 0
        ),
        axis=1,
    )

    packed = streamed(
        pack_kernel,
        [(1, 4), (1, 4), (owned, window), (owned, columns)],
        (dp, owned, window + columns + LANES),
    )(
        prompt_of_block.reshape(1, -1),
        reward_of_block.reshape(1, -1),
        adapter_down_factors,
        adapter_up_factors,
    )
    gathered = lax.all_to_all(packed, "dp", 0, 0)

    cotangent = jnp.transpose(key_value_cotangent, (1, 0, 2))
    steps = jnp.array([[1, 0], [1, 1], [2, 0], [3, 0], [3, 1], [2, 1], [0, 0], [0, 1]], jnp.int32)
    targets = (chip + steps[:, 0]) % CHIPS * 2 + (core + steps[:, 1]) % 2
    to_next, next_other, to_prev, prev_other, mine, other = payloads(
        targets * 4 + x, key_value_weight, cotangent, tile
    )
    before, after = tensor_send(to_next, 1, 0), tensor_send(to_prev, 3, 0)
    before_other, after_other = tensor_send(next_other, 1, 1), tensor_send(prev_other, 3, 1)
    partner = tensor_send(other, 0, 1)
    unit = 2 * tile
    hop_next, hop_prev = lax.optimization_barrier((before[unit : 3 * unit], after[2 * unit :]))
    hop_next, hop_prev = tensor_send(hop_next, 1, 0), tensor_send(hop_prev, 3, 1)
    slabs = assemble(
        *[(piece, 0, unit) for piece in (mine, before, after, hop_next)],
        *[(piece, 0, unit) for piece in (partner, before_other, after_other)],
        (hop_prev, unit, 2 * unit),
    )
    cots = assemble(
        (cotangent.reshape(2 * rows, columns), 0, 2 * rows),
        (before, 2 * unit, 4 * unit),
        (after, unit, 3 * unit),
        (hop_next, unit, 2 * unit),
        (hop_prev, 0, unit),
    )
    gathered, slabs, cots = lax.optimization_barrier((gathered, slabs, cots))

    low, weighted_value, coef = call(
        low_kernel,
        [SMEM] * 4 + [VMEM] * 3,
        [shape((rows, 2 * RANK), F32), shape((rows, columns), BF), shape((rows, 1), F32)],
        2 * rows * RANK * window,
        16,
    )(
        slots,
        live_rows_of_block,
        prompt_of_block,
        reward_of_block,
        gathered,
        normed_input_rows,
        cotangent,
    )
    low = (low + tensor_send(low, 0, 1)).astype(BF)
    lows = [low] + [tensor_send(low, s, 0) for s in (1, 3, 2)]
    slabs_left, slabs_right = x_send(slabs, 1), x_send(slabs, 3)

    terms, low = call(
        terms_kernel,
        [SMEM] + [VMEM] * 6,
        [shape((dp, owned, window + columns), BF), shape((rows, 2 * RANK), BF)],
        4 * rows * RANK * window,
        16,
    )(slots, *lows, normed_input_rows, weighted_value)
    cots_other = tensor_send(cots, 0, 1)
    terms, slabs_left, slabs_right, cots, cots_other = lax.optimization_barrier(
        (terms, slabs_left, slabs_right, cots, cots_other)
    )
    terms = lax.all_to_all(terms, "dp", 0, 0)
    half = slabs.shape[0] // 2
    slabs_far = (x_send(slabs_left[:half], 1), x_send(slabs_right[half:], 3))
    quarters = (x + jnp.array([0, 3, 1, 2], jnp.int32)) % 4
    input_gradient = frozen_and_correction(
        slots,
        quarters,
        (cots, cots_other),
        (gathered, low, coef),
        (slabs, slabs_left, slabs_right),
        slabs_far,
        window,
    )
    grad_a, grad_b = call(
        sum_kernel,
        [VMEM],
        [shape((owned, window), F32), shape((owned, columns), F32)],
        0,
        8,
    )(terms)
    return (input_gradient, grad_a, grad_b)


def solution(mesh):
    in_specs = (
        P("dp", "tensor"),
        P("dp", None, "tensor"),
        P(None, None, "tensor"),
        P("dp", "tensor"),
        P("dp", "tensor"),
        P(),
        P("dp"),
        P("dp"),
        P("dp"),
        P("dp"),
    )
    out_specs = (P("dp", "tensor"), P("dp", "tensor"), P("dp", "tensor"))
    return jax.shard_map(shards, mesh=mesh, in_specs=in_specs, out_specs=out_specs, check_vma=False)
```

```python
import functools

import jax
import jax.numpy as jnp
from jax import lax
from jax.experimental import pallas as pl
from jax.experimental.pallas import tpu as pltpu
from jax.sharding import PartitionSpec as P

BLOCK = 128
GSIZE = 8
SLOTS = 8
RANK = 64
LANES = 128
CHIPS = 4
FULL_VMEM = 60 * 2**20
LOWRANK_MULTIPLIER = 2.0
BF = jnp.bfloat16
F32 = jnp.float32
VMEM = pl.BlockSpec(memory_space=pltpu.VMEM)
SMEM = pl.BlockSpec(memory_space=pltpu.SMEM)


def dot(a, b, ca, cb):
    return lax.dot_general(a, b, (((ca,), (cb,)), ((), ())), preferred_element_type=F32)


def call(kernel, in_specs, shapes, flops, mib):
    single = not isinstance(shapes, (list, tuple))
    shapes = [shapes] if single else list(shapes)
    return pl.pallas_call(
        kernel,
        in_specs=in_specs,
        out_specs=VMEM if single else [VMEM] * len(shapes),
        out_shape=shapes[0] if single else shapes,
        compiler_params=pltpu.CompilerParams(vmem_limit_bytes=mib * 2**20),
        cost_estimate=pl.CostEstimate(flops=flops, bytes_accessed=2**20, transcendentals=0),
    )


def tensor_send(value, chip_step, core_flip):
    pairs = [
        (y * 2 + c, (y + chip_step) % CHIPS * 2 + (c ^ core_flip))
        for y in range(CHIPS)
        for c in range(2)
    ]
    return lax.ppermute(value, "tensor", pairs)


def x_send(value, step):
    pairs = [(i, i // 4 * 4 + (i + step) % 4) for i in range(lax.axis_size("dp"))]
    return lax.ppermute(value, "dp", pairs)


def pack_kernel(prompt, reward, down_ref, up_ref, out_ref):
    shape = (down_ref.shape[0], LANES)
    row = lax.broadcasted_iota(jnp.int32, shape, 0)
    lane = lax.broadcasted_iota(jnp.int32, shape, 1)
    blocks = reward.shape[1]
    rewards = jnp.zeros(shape, F32)
    prompts = jnp.full(shape, -1.0, F32)
    for b in range(blocks):
        one = (slice(0, 1), slice(b, b + 1))
        rewards = jnp.where(lane % blocks == b, reward[one], rewards)
        prompts = jnp.where(lane == b, prompt[one].astype(F32), prompts)
    high = rewards.astype(BF).astype(F32)
    rest = rewards - high
    middle = rest.astype(BF).astype(F32)
    part = lane // blocks
    parts = jnp.where(part == 0, high, jnp.where(part == 1, middle, rest - middle))
    parts = jnp.where(part < 3, parts, 0.0)
    facts = jnp.where(row == 0, parts, jnp.where(row == 1, prompts, 0.0)).astype(BF)
    packed = jnp.concatenate([down_ref[...], up_ref[...], facts], axis=1)
    for i in range(out_ref.shape[0]):
        out_ref[i] = packed


def streamed(kernel, blocks, out):
    whole = lambda shape: pl.BlockSpec(shape, lambda i: (0,) * len(shape))
    return pl.pallas_call(
        kernel,
        grid=(1,),
        in_specs=[whole(shape) for shape in blocks],
        out_specs=whole(out),
        out_shape=jax.ShapeDtypeStruct(out, BF),
        compiler_params=pltpu.CompilerParams(vmem_limit_bytes=FULL_VMEM),
    )


def assemble_kernel(cuts, *refs):
    *pieces, out_ref = refs
    at = 0
    for piece, (start, stop) in zip(pieces, cuts, strict=True):
        out_ref[at : at + stop - start] = piece[start:stop]
        at += stop - start


def assemble(*pieces):
    arrays = [p[0] for p in pieces]
    cuts = [p[1:] for p in pieces]
    columns = arrays[0].shape[1]
    total = sum(stop - start for start, stop in cuts)
    whole = lambda shape: pl.BlockSpec(shape, lambda i: (0,) * len(shape))
    return pl.pallas_call(
        functools.partial(assemble_kernel, cuts),
        grid=(1,),
        in_specs=[whole(v.shape) for v in arrays],
        out_specs=whole((total, columns)),
        out_shape=jax.ShapeDtypeStruct((total, columns), BF),
        compiler_params=pltpu.CompilerParams(vmem_limit_bytes=24 * 2**20),
    )(*arrays)


def payload_kernel(places, *refs):
    *slabs, cot_ref, next_ref, next_other, prev_ref, prev_other, mine_ref, other_ref = refs
    tile, rows = slabs[0].shape[1], cot_ref.shape[1]
    key, value = (cot_ref.at[0],), (cot_ref.at[1],)
    slab = lambda i: (slabs[i].at[0], slabs[i].at[1])
    orders = (
        (next_ref, (slab(0), slab(2), key, value)),
        (next_other, (slab(1),)),
        (prev_ref, (slab(3), key, value, slab(5))),
        (prev_other, (slab(4),)),
        (mine_ref, (slab(6),)),
        (other_ref, (slab(7),)),
    )
    for out_ref, units in orders:
        at = 0
        for piece in (p for unit in units for p in unit):
            out_ref[at : at + piece.shape[0]] = piece[...]
            at += piece.shape[0]


def payloads(places, weight, cotangent, tile):
    columns = weight.shape[2]
    slab = [
        pl.BlockSpec((2, tile, columns), lambda g, p, i=i: (0, p[i], 0)) for i in range(8)
    ]
    sizes = [n * 2 * tile for n in (4, 1, 4, 1, 1, 1)]
    return pl.pallas_call(
        payload_kernel,
        grid_spec=pltpu.PrefetchScalarGridSpec(
            num_scalar_prefetch=1,
            grid=(1,),
            in_specs=[*slab, pl.BlockSpec(cotangent.shape, lambda g, p: (0, 0, 0))],
            out_specs=[pl.BlockSpec((n, columns), lambda g, p: (0, 0)) for n in sizes],
        ),
        out_shape=[jax.ShapeDtypeStruct((n, columns), BF) for n in sizes],
        compiler_params=pltpu.CompilerParams(vmem_limit_bytes=FULL_VMEM),
    )(places, *[weight] * 8, cotangent)


def factor_rows(ref, slot, start, size):
    owners = ref.shape[0] // SLOTS
    return ref[pl.ds(slot * owners, owners), :, pl.ds(start, size)].reshape(RANK, size)


def low_kernel(
    slots, live, prompt, reward, gathered_ref, x_ref, cot_ref, low_ref, weighted_ref, coef_ref
):
    window = x_ref.shape[1]
    columns = cot_ref.shape[2]
    blocks = reward.shape[0]
    facts = gathered_ref[:, :, window + columns :].astype(F32)
    row = lax.broadcasted_iota(jnp.int32, facts.shape, 1)
    parts = jnp.sum(jnp.where(row == 0, facts, 0.0), axis=1)
    prompts = jnp.sum(jnp.where(row == 1, facts, 0.0), axis=1)
    rewards = parts + pltpu.roll(parts, LANES - blocks, 1)
    rewards = rewards + pltpu.roll(parts, LANES - 2 * blocks, 1)
    place = lax.broadcasted_iota(jnp.int32, (BLOCK, 1), 0)
    whole = lambda v: jnp.sum(jnp.sum(v, axis=1, keepdims=True), axis=0, keepdims=True)
    for b in range(blocks):
        same = prompts == prompt[b].astype(F32)
        mean = whole(jnp.where(same, rewards, 0.0)) / GSIZE
        square = whole(jnp.where(same, rewards * rewards, 0.0)) / GSIZE
        spread = jnp.sqrt(jnp.maximum(square - mean * mean, 1.0))
        advantage = (reward[b] - mean) / spread
        coef = jnp.where(place < live[b], -advantage / GSIZE, 0.0)
        rows = pl.ds(b * BLOCK, BLOCK)
        weighted = (cot_ref[1, rows, :].astype(F32) * coef).astype(BF)
        low_h = dot(x_ref[rows, :], factor_rows(gathered_ref, slots[b], 0, window), 1, 1)
        low_g = dot(weighted, factor_rows(gathered_ref, slots[b], window, columns), 1, 1)
        low_ref[rows, :] = jnp.concatenate([low_h, low_g], axis=1)
        weighted_ref[rows, :] = weighted
        coef_ref[rows, :] = coef


def terms_kernel(slots, own, first, second, third, x_ref, weighted_ref, terms_ref, low_ref):
    window = x_ref.shape[1]
    columns = weighted_ref.shape[1]
    owners, owned = terms_ref.shape[0] // SLOTS, terms_ref.shape[1]
    low = own[...].astype(F32) + first[...].astype(F32)
    low = (low + second[...].astype(F32)) + third[...].astype(F32)
    low_ref[...] = low.astype(BF)
    for i in range(terms_ref.shape[0]):
        terms_ref[i] = jnp.zeros(terms_ref.shape[1:], BF)
    for b in range(x_ref.shape[0] // BLOCK):
        rows = pl.ds(b * BLOCK, BLOCK)
        low = low_ref[rows, :]
        down = LOWRANK_MULTIPLIER * dot(low, x_ref[rows, :], 0, 0)[RANK:]
        up = LOWRANK_MULTIPLIER * dot(low, weighted_ref[rows, :], 0, 0)[:RANK]
        place = pl.ds(slots[b] * owners, owners)
        terms_ref[place, :, :window] = down.astype(BF).reshape(owners, owned, window)
        terms_ref[place, :, window:] = up.astype(BF).reshape(owners, owned, columns)


def quarter(weighted, parts, low_ref, gathered_ref, slots, start, tile):
    slabs = [p[i * tile : (i + 1) * tile] for p in parts for i in range(p.shape[0] // tile)]
    total = dot(weighted[...], jnp.concatenate(slabs, axis=1), 1, 1)
    extra = []
    for b in range(total.shape[0] // BLOCK):
        factor = factor_rows(gathered_ref, slots[b], start, tile)
        factor = jnp.concatenate([jnp.zeros_like(factor), factor], axis=0)
        low = low_ref[b * BLOCK : (b + 1) * BLOCK, :]
        extra.append(LOWRANK_MULTIPLIER * dot(low, factor, 1, 0))
    return (total + jnp.concatenate(extra, axis=0)).astype(BF)


def near_kernel(slots, quarters, cots, others, gathered_ref, low_ref, coef_ref, *refs):
    *slabs, out_ref, weighted = refs
    rows, columns = coef_ref.shape[0], cots.shape[1]
    tile = rows // 2
    coef = coef_ref[...]
    count = cots.shape[0] // rows
    for i in range(2 * count):
        source = (cots, others)[(i // count + (i % count == count - 1)) % 2]
        piece = source[i % count * rows : (i % count + 1) * rows]
        weighted[:, i * columns : (i + 1) * columns] = (piece.astype(F32) * coef).astype(BF)
    for r, part in enumerate(slabs):
        start = pl.multiple_of(quarters[r] * tile, tile)
        out_ref[:, pl.ds(start, tile)] = quarter(
            weighted, (part,), low_ref, gathered_ref, slots, start, tile
        )


def far_kernel(slots, quarters, near_ref, weighted, gathered_ref, low_ref, *refs):
    *parts, out_ref = refs
    tile = out_ref.shape[1]
    parts = [ref.at[pl.ds(0, 2 * tile)] for ref in parts]
    out_ref[...] = quarter(weighted, parts, low_ref, gathered_ref, slots, 0, tile)


def frozen_and_correction(slots, quarters, cots, adapter, near, far, window):
    gathered, low, coef = adapter
    rows, columns, tile = coef.shape[0], cots[0].shape[1], window // 4
    depth = 2 * cots[0].shape[0] // rows * columns
    shape = jax.ShapeDtypeStruct
    whole = lambda dims: pl.BlockSpec(dims, lambda i, *_: (0,) * len(dims))
    streams = [*cots, gathered, low, coef, *near]
    partial, weighted = pl.pallas_call(
        near_kernel,
        grid_spec=pltpu.PrefetchScalarGridSpec(
            num_scalar_prefetch=2,
            grid=(1,),
            in_specs=[whole(v.shape) for v in streams],
            out_specs=[whole((rows, window)), whole((rows, depth))],
        ),
        out_shape=[shape((rows, window), BF), shape((rows, depth), BF)],
        compiler_params=pltpu.CompilerParams(vmem_limit_bytes=FULL_VMEM // 2),
    )(slots, quarters, *streams)
    owners, owned = gathered.shape[:2]
    return pl.pallas_call(
        far_kernel,
        grid_spec=pltpu.PrefetchScalarGridSpec(
            num_scalar_prefetch=2,
            grid=(1,),
            in_specs=[
                pl.BlockSpec(memory_space=pl.ANY),
                whole(weighted.shape),
                pl.BlockSpec((owners, owned, tile), lambda i, s, q: (0, 0, q[3])),
                whole(low.shape),
                *[whole(v.shape) for v in far],
            ],
            out_specs=pl.BlockSpec((rows, tile), lambda i, s, q: (0, q[3])),
        ),
        out_shape=shape((rows, window), BF),
        input_output_aliases={2: 0},
        compiler_params=pltpu.CompilerParams(vmem_limit_bytes=FULL_VMEM // 2),
    )(slots, quarters, partial, weighted, gathered, low, *far)


def sum_kernel(terms_ref, down_ref, up_ref):
    window = down_ref.shape[1]
    total = terms_ref[0].astype(F32)
    for i in range(1, terms_ref.shape[0]):
        total = total + terms_ref[i].astype(F32)
    down_ref[...] = total[:, :window]
    up_ref[...] = total[:, window:]


def shards(
    normed_input_rows,
    key_value_cotangent,
    key_value_weight,
    adapter_down_factors,
    adapter_up_factors,
    slot_adapter,
    adapter_of_block,
    live_rows_of_block,
    prompt_of_block,
    reward_of_block,
):
    rows, window = normed_input_rows.shape
    columns = key_value_cotangent.shape[2]
    dp = lax.axis_size("dp")
    owned = adapter_down_factors.shape[0]
    te = lax.axis_index("tensor")
    chip, core = te // 2, te % 2
    x = lax.axis_index("dp") % 4
    tile = window // 4
    shape = jax.ShapeDtypeStruct
    slots = jnp.sum(
        jnp.where(
            adapter_of_block[:, None] == slot_adapter[None, :], jnp.arange(SLOTS, dtype=jnp.int32), 0
        ),
        axis=1,
    )

    packed = streamed(
        pack_kernel,
        [(1, 4), (1, 4), (owned, window), (owned, columns)],
        (dp, owned, window + columns + LANES),
    )(
        prompt_of_block.reshape(1, -1),
        reward_of_block.reshape(1, -1),
        adapter_down_factors,
        adapter_up_factors,
    )
    gathered = lax.all_to_all(packed, "dp", 0, 0)

    cotangent = jnp.transpose(key_value_cotangent, (1, 0, 2))
    steps = jnp.array([[1, 0], [1, 1], [2, 0], [3, 0], [3, 1], [2, 1], [0, 0], [0, 1]], jnp.int32)
    targets = (chip + steps[:, 0]) % CHIPS * 2 + (core + steps[:, 1]) % 2
    to_next, next_other, to_prev, prev_other, mine, other = payloads(
        targets * 4 + x, key_value_weight, cotangent, tile
    )
    before, after = tensor_send(to_next, 1, 0), tensor_send(to_prev, 3, 0)
    before_other, after_other = tensor_send(next_other, 1, 1), tensor_send(prev_other, 3, 1)
    partner = tensor_send(other, 0, 1)
    unit = 2 * tile
    hop_next, hop_prev = lax.optimization_barrier((before[unit : 3 * unit], after[2 * unit :]))
    hop_next, hop_prev = tensor_send(hop_next, 1, 0), tensor_send(hop_prev, 3, 1)
    slabs = assemble(
        *[(piece, 0, unit) for piece in (mine, before, after, hop_next)],
        *[(piece, 0, unit) for piece in (partner, before_other, after_other)],
        (hop_prev, unit, 2 * unit),
    )
    cots = assemble(
        (cotangent.reshape(2 * rows, columns), 0, 2 * rows),
        (before, 2 * unit, 4 * unit),
        (after, unit, 3 * unit),
        (hop_next, unit, 2 * unit),
        (hop_prev, 0, unit),
    )
    gathered, slabs, cots, weight = lax.optimization_barrier(
        (gathered, slabs, cots, key_value_weight)
    )

    def across(chip_step, core_flip):
        target = (chip + chip_step) % CHIPS * 2 + (core + core_flip) % 2
        start = target * window + (x + 2) % 4 * tile
        return lax.dynamic_slice_in_dim(weight, start, tile, 1).reshape(unit, columns)

    late = [
        jnp.concatenate([across(1, 0), across(2, 0)]),
        jnp.concatenate([across(3, 0), across(2, 1)]),
        *[across(*step) for step in ((1, 1), (3, 1), (0, 1), (0, 0))],
    ]

    low, weighted_value, coef = call(
        low_kernel,
        [SMEM] * 4 + [VMEM] * 3,
        [shape((rows, 2 * RANK), F32), shape((rows, columns), BF), shape((rows, 1), F32)],
        2 * rows * RANK * window,
        16,
    )(
        slots,
        live_rows_of_block,
        prompt_of_block,
        reward_of_block,
        gathered,
        normed_input_rows,
        cotangent,
    )
    low = (low + tensor_send(low, 0, 1)).astype(BF)
    lows = [low] + [tensor_send(low, s, 0) for s in (1, 3, 2)]
    slabs_left, slabs_right = x_send(slabs, 1), x_send(slabs, 3)

    terms, low = call(
        terms_kernel,
        [SMEM] + [VMEM] * 6,
        [shape((dp, owned, window + columns), BF), shape((rows, 2 * RANK), BF)],
        4 * rows * RANK * window,
        16,
    )(slots, *lows, normed_input_rows, weighted_value)
    cots_other = tensor_send(cots, 0, 1)
    terms, slabs_left, slabs_right, cots, cots_other, late = lax.optimization_barrier(
        (terms, slabs_left, slabs_right, cots, cots_other, late)
    )
    terms = lax.all_to_all(terms, "dp", 0, 0)
    routes = (1, 0), (3, 0), (1, 1), (3, 1), (0, 1)
    before, after, before_other, after_other, partner = [
        tensor_send(v, *route) for v, route in zip(late[:5], routes, strict=True)
    ]
    hop_next, hop_prev = lax.optimization_barrier((before[unit:], after[unit:]))
    slabs_far = [
        late[5], before, after, tensor_send(hop_next, 1, 0),
        partner, before_other, after_other, tensor_send(hop_prev, 3, 1),
    ]
    quarters = (x + jnp.array([0, 3, 1, 2], jnp.int32)) % 4
    input_gradient = frozen_and_correction(
        slots,
        quarters,
        (cots, cots_other),
        (gathered, low, coef),
        (slabs, slabs_left, slabs_right),
        slabs_far,
        window,
    )
    grad_a, grad_b = call(
        sum_kernel,
        [VMEM],
        [shape((owned, window), F32), shape((owned, columns), F32)],
        0,
        8,
    )(terms)
    return (input_gradient, grad_a, grad_b)


def solution(mesh):
    in_specs = (
        P("dp", "tensor"),
        P("dp", None, "tensor"),
        P(None, None, "tensor"),
        P("dp", "tensor"),
        P("dp", "tensor"),
        P(),
        P("dp"),
        P("dp"),
        P("dp"),
        P("dp"),
    )
    out_specs = (P("dp", "tensor"), P("dp", "tensor"), P("dp", "tensor"))
    return jax.shard_map(shards, mesh=mesh, in_specs=in_specs, out_specs=out_specs, check_vma=False)
```

```python
import functools

import jax
import jax.numpy as jnp
from jax import lax
from jax.experimental import pallas as pl
from jax.experimental.pallas import tpu as pltpu
from jax.sharding import PartitionSpec as P

BLOCK = 128
GSIZE = 8
SLOTS = 8
RANK = 64
LANES = 128
CHIPS = 4
FULL_VMEM = 60 * 2**20
LOWRANK_MULTIPLIER = 2.0
BF = jnp.bfloat16
F32 = jnp.float32
VMEM = pl.BlockSpec(memory_space=pltpu.VMEM)
SMEM = pl.BlockSpec(memory_space=pltpu.SMEM)


def dot(a, b, ca, cb):
    return lax.dot_general(a, b, (((ca,), (cb,)), ((), ())), preferred_element_type=F32)


def call(kernel, in_specs, shapes, flops, mib):
    single = not isinstance(shapes, (list, tuple))
    shapes = [shapes] if single else list(shapes)
    return pl.pallas_call(
        kernel,
        in_specs=in_specs,
        out_specs=VMEM if single else [VMEM] * len(shapes),
        out_shape=shapes[0] if single else shapes,
        compiler_params=pltpu.CompilerParams(vmem_limit_bytes=mib * 2**20),
        cost_estimate=pl.CostEstimate(flops=flops, bytes_accessed=2**20, transcendentals=0),
    )


def tensor_send(value, chip_step, core_flip):
    pairs = [
        (y * 2 + c, (y + chip_step) % CHIPS * 2 + (c ^ core_flip))
        for y in range(CHIPS)
        for c in range(2)
    ]
    return lax.ppermute(value, "tensor", pairs)


def x_send(value, step):
    pairs = [(i, i // 4 * 4 + (i + step) % 4) for i in range(lax.axis_size("dp"))]
    return lax.ppermute(value, "dp", pairs)


def pack_kernel(prompt, reward, down_ref, up_ref, out_ref):
    shape = (down_ref.shape[0], LANES)
    row = lax.broadcasted_iota(jnp.int32, shape, 0)
    lane = lax.broadcasted_iota(jnp.int32, shape, 1)
    blocks = reward.shape[1]
    rewards = jnp.zeros(shape, F32)
    prompts = jnp.full(shape, -1.0, F32)
    for b in range(blocks):
        one = (slice(0, 1), slice(b, b + 1))
        rewards = jnp.where(lane % blocks == b, reward[one], rewards)
        prompts = jnp.where(lane == b, prompt[one].astype(F32), prompts)
    high = rewards.astype(BF).astype(F32)
    rest = rewards - high
    middle = rest.astype(BF).astype(F32)
    part = lane // blocks
    parts = jnp.where(part == 0, high, jnp.where(part == 1, middle, rest - middle))
    parts = jnp.where(part < 3, parts, 0.0)
    facts = jnp.where(row == 0, parts, jnp.where(row == 1, prompts, 0.0)).astype(BF)
    packed = jnp.concatenate([down_ref[...], up_ref[...], facts], axis=1)
    for i in range(out_ref.shape[0]):
        out_ref[i] = packed


def streamed(kernel, blocks, out):
    whole = lambda shape: pl.BlockSpec(shape, lambda i: (0,) * len(shape))
    return pl.pallas_call(
        kernel,
        grid=(1,),
        in_specs=[whole(shape) for shape in blocks],
        out_specs=whole(out),
        out_shape=jax.ShapeDtypeStruct(out, BF),
        compiler_params=pltpu.CompilerParams(vmem_limit_bytes=FULL_VMEM),
    )


def assemble_kernel(cuts, *refs):
    *pieces, out_ref = refs
    at = 0
    for piece, (start, stop) in zip(pieces, cuts, strict=True):
        out_ref[at : at + stop - start] = piece[start:stop]
        at += stop - start


def assemble(*pieces):
    arrays = [p[0] for p in pieces]
    cuts = [p[1:] for p in pieces]
    columns = arrays[0].shape[1]
    total = sum(stop - start for start, stop in cuts)
    whole = lambda shape: pl.BlockSpec(shape, lambda i: (0,) * len(shape))
    return pl.pallas_call(
        functools.partial(assemble_kernel, cuts),
        grid=(1,),
        in_specs=[whole(v.shape) for v in arrays],
        out_specs=whole((total, columns)),
        out_shape=jax.ShapeDtypeStruct((total, columns), BF),
        compiler_params=pltpu.CompilerParams(vmem_limit_bytes=24 * 2**20),
    )(*arrays)


def payload_kernel(places, *refs):
    *slabs, cot_ref, next_ref, next_other, prev_ref, prev_other, mine_ref, other_ref = refs
    tile, rows = slabs[0].shape[1], cot_ref.shape[1]
    key, value = (cot_ref.at[0],), (cot_ref.at[1],)
    slab = lambda i: (slabs[i].at[0], slabs[i].at[1])
    orders = (
        (next_ref, (slab(0), slab(2), key, value)),
        (next_other, (slab(1),)),
        (prev_ref, (slab(3), key, value, slab(5))),
        (prev_other, (slab(4),)),
        (mine_ref, (slab(6),)),
        (other_ref, (slab(7),)),
    )
    for out_ref, units in orders:
        at = 0
        for piece in (p for unit in units for p in unit):
            out_ref[at : at + piece.shape[0]] = piece[...]
            at += piece.shape[0]


def payloads(places, weight, cotangent, tile):
    columns = weight.shape[2]
    slab = [
        pl.BlockSpec((2, tile, columns), lambda g, p, i=i: (0, p[i], 0)) for i in range(8)
    ]
    sizes = [n * 2 * tile for n in (4, 1, 4, 1, 1, 1)]
    return pl.pallas_call(
        payload_kernel,
        grid_spec=pltpu.PrefetchScalarGridSpec(
            num_scalar_prefetch=1,
            grid=(1,),
            in_specs=[*slab, pl.BlockSpec(cotangent.shape, lambda g, p: (0, 0, 0))],
            out_specs=[pl.BlockSpec((n, columns), lambda g, p: (0, 0)) for n in sizes],
        ),
        out_shape=[jax.ShapeDtypeStruct((n, columns), BF) for n in sizes],
        compiler_params=pltpu.CompilerParams(vmem_limit_bytes=FULL_VMEM),
    )(places, *[weight] * 8, cotangent)


def factor_rows(ref, slot, start, size):
    owners = ref.shape[0] // SLOTS
    return ref[pl.ds(slot * owners, owners), :, pl.ds(start, size)].reshape(RANK, size)


def low_kernel(
    slots, live, prompt, reward, gathered_ref, x_ref, cot_ref, low_ref, weighted_ref, coef_ref
):
    window = x_ref.shape[1]
    columns = cot_ref.shape[2]
    blocks = reward.shape[0]
    facts = gathered_ref[:, :, window + columns :].astype(F32)
    row = lax.broadcasted_iota(jnp.int32, facts.shape, 1)
    parts = jnp.sum(jnp.where(row == 0, facts, 0.0), axis=1)
    prompts = jnp.sum(jnp.where(row == 1, facts, 0.0), axis=1)
    rewards = parts + pltpu.roll(parts, LANES - blocks, 1)
    rewards = rewards + pltpu.roll(parts, LANES - 2 * blocks, 1)
    place = lax.broadcasted_iota(jnp.int32, (BLOCK, 1), 0)
    whole = lambda v: jnp.sum(jnp.sum(v, axis=1, keepdims=True), axis=0, keepdims=True)
    for b in range(blocks):
        same = prompts == prompt[b].astype(F32)
        mean = whole(jnp.where(same, rewards, 0.0)) / GSIZE
        square = whole(jnp.where(same, rewards * rewards, 0.0)) / GSIZE
        spread = jnp.sqrt(jnp.maximum(square - mean * mean, 1.0))
        advantage = (reward[b] - mean) / spread
        coef = jnp.where(place < live[b], -advantage / GSIZE, 0.0)
        rows = pl.ds(b * BLOCK, BLOCK)
        weighted = (cot_ref[1, rows, :].astype(F32) * coef).astype(BF)
        low_h = dot(x_ref[rows, :], factor_rows(gathered_ref, slots[b], 0, window), 1, 1)
        low_g = dot(weighted, factor_rows(gathered_ref, slots[b], window, columns), 1, 1)
        low_ref[rows, :] = jnp.concatenate([low_h, low_g], axis=1)
        weighted_ref[rows, :] = weighted
        coef_ref[rows, :] = coef


def terms_kernel(slots, own, first, second, third, x_ref, weighted_ref, terms_ref, low_ref):
    window = x_ref.shape[1]
    columns = weighted_ref.shape[1]
    owners, owned = terms_ref.shape[0] // SLOTS, terms_ref.shape[1]
    low = own[...].astype(F32) + first[...].astype(F32)
    low = (low + second[...].astype(F32)) + third[...].astype(F32)
    low_ref[...] = low.astype(BF)
    for i in range(terms_ref.shape[0]):
        terms_ref[i] = jnp.zeros(terms_ref.shape[1:], BF)
    for b in range(x_ref.shape[0] // BLOCK):
        rows = pl.ds(b * BLOCK, BLOCK)
        low = low_ref[rows, :]
        down = LOWRANK_MULTIPLIER * dot(low, x_ref[rows, :], 0, 0)[RANK:]
        up = LOWRANK_MULTIPLIER * dot(low, weighted_ref[rows, :], 0, 0)[:RANK]
        place = pl.ds(slots[b] * owners, owners)
        terms_ref[place, :, :window] = down.astype(BF).reshape(owners, owned, window)
        terms_ref[place, :, window:] = up.astype(BF).reshape(owners, owned, columns)


def quarter(weighted, parts, low_ref, gathered_ref, slots, start, tile):
    slabs = [p[i * tile : (i + 1) * tile] for p in parts for i in range(p.shape[0] // tile)]
    total = dot(weighted[...], jnp.concatenate(slabs, axis=1), 1, 1)
    extra = []
    for b in range(total.shape[0] // BLOCK):
        factor = factor_rows(gathered_ref, slots[b], start, tile)
        factor = jnp.concatenate([jnp.zeros_like(factor), factor], axis=0)
        low = low_ref[b * BLOCK : (b + 1) * BLOCK, :]
        extra.append(LOWRANK_MULTIPLIER * dot(low, factor, 1, 0))
    return (total + jnp.concatenate(extra, axis=0)).astype(BF)


def near_kernel(slots, quarters, cots, others, gathered_ref, low_ref, coef_ref, *refs):
    *slabs, out_ref, weighted = refs
    rows, columns = coef_ref.shape[0], cots.shape[1]
    tile = rows // 2
    coef = coef_ref[...]
    count = cots.shape[0] // rows
    for i in range(2 * count):
        source = (cots, others)[(i // count + (i % count == count - 1)) % 2]
        piece = source[i % count * rows : (i % count + 1) * rows]
        weighted[:, i * columns : (i + 1) * columns] = (piece.astype(F32) * coef).astype(BF)
    for r, pair in enumerate(zip(slabs[::2], slabs[1::2], strict=True)):
        start = pl.multiple_of(quarters[r] * tile, tile)
        out_ref[:, pl.ds(start, tile)] = quarter(
            weighted, pair, low_ref, gathered_ref, slots, start, tile
        )


def far_kernel(slots, quarters, near_ref, weighted, gathered_ref, low_ref, *refs):
    *parts, out_ref = refs
    tile = out_ref.shape[1]
    parts = [ref.at[pl.ds(0, 2 * tile)] for ref in parts]
    out_ref[...] = quarter(weighted, parts, low_ref, gathered_ref, slots, 0, tile)


def frozen_and_correction(slots, quarters, cots, adapter, near, far, window):
    gathered, low, coef = adapter
    rows, columns, tile = coef.shape[0], cots[0].shape[1], window // 4
    depth = 2 * cots[0].shape[0] // rows * columns
    shape = jax.ShapeDtypeStruct
    whole = lambda dims: pl.BlockSpec(dims, lambda i, *_: (0,) * len(dims))
    streams = [*cots, gathered, low, coef, *near]
    partial, weighted = pl.pallas_call(
        near_kernel,
        grid_spec=pltpu.PrefetchScalarGridSpec(
            num_scalar_prefetch=2,
            grid=(1,),
            in_specs=[whole(v.shape) for v in streams],
            out_specs=[whole((rows, window)), whole((rows, depth))],
        ),
        out_shape=[shape((rows, window), BF), shape((rows, depth), BF)],
        compiler_params=pltpu.CompilerParams(vmem_limit_bytes=FULL_VMEM // 2),
    )(slots, quarters, *streams)
    owners, owned = gathered.shape[:2]
    return pl.pallas_call(
        far_kernel,
        grid_spec=pltpu.PrefetchScalarGridSpec(
            num_scalar_prefetch=2,
            grid=(1,),
            in_specs=[
                pl.BlockSpec(memory_space=pl.ANY),
                whole(weighted.shape),
                pl.BlockSpec((owners, owned, tile), lambda i, s, q: (0, 0, q[3])),
                whole(low.shape),
                *[whole(v.shape) for v in far],
            ],
            out_specs=pl.BlockSpec((rows, tile), lambda i, s, q: (0, q[3])),
        ),
        out_shape=shape((rows, window), BF),
        input_output_aliases={2: 0},
        compiler_params=pltpu.CompilerParams(vmem_limit_bytes=FULL_VMEM // 2),
    )(slots, quarters, partial, weighted, gathered, low, *far)


def sum_kernel(terms_ref, down_ref, up_ref):
    window = down_ref.shape[1]
    total = terms_ref[0].astype(F32)
    for i in range(1, terms_ref.shape[0]):
        total = total + terms_ref[i].astype(F32)
    down_ref[...] = total[:, :window]
    up_ref[...] = total[:, window:]


def shards(
    normed_input_rows,
    key_value_cotangent,
    key_value_weight,
    adapter_down_factors,
    adapter_up_factors,
    slot_adapter,
    adapter_of_block,
    live_rows_of_block,
    prompt_of_block,
    reward_of_block,
):
    rows, window = normed_input_rows.shape
    columns = key_value_cotangent.shape[2]
    dp = lax.axis_size("dp")
    owned = adapter_down_factors.shape[0]
    te = lax.axis_index("tensor")
    chip, core = te // 2, te % 2
    x = lax.axis_index("dp") % 4
    tile = window // 4
    shape = jax.ShapeDtypeStruct
    slots = jnp.sum(
        jnp.where(
            adapter_of_block[:, None] == slot_adapter[None, :], jnp.arange(SLOTS, dtype=jnp.int32), 0
        ),
        axis=1,
    )

    packed = streamed(
        pack_kernel,
        [(1, 4), (1, 4), (owned, window), (owned, columns)],
        (dp, owned, window + columns + LANES),
    )(
        prompt_of_block.reshape(1, -1),
        reward_of_block.reshape(1, -1),
        adapter_down_factors,
        adapter_up_factors,
    )
    gathered = lax.all_to_all(packed, "dp", 0, 0)

    cotangent = jnp.transpose(key_value_cotangent, (1, 0, 2))
    steps = jnp.array([[1, 0], [1, 1], [2, 0], [3, 0], [3, 1], [2, 1], [0, 0], [0, 1]], jnp.int32)
    targets = (chip + steps[:, 0]) % CHIPS * 2 + (core + steps[:, 1]) % 2
    to_next, next_other, to_prev, prev_other, mine, other = payloads(
        targets * 4 + x, key_value_weight, cotangent, tile
    )
    before, after = tensor_send(to_next, 1, 0), tensor_send(to_prev, 3, 0)
    before_other, after_other = tensor_send(next_other, 1, 1), tensor_send(prev_other, 3, 1)
    partner = tensor_send(other, 0, 1)
    unit = 2 * tile
    hop_next, hop_prev = lax.optimization_barrier((before[unit : 3 * unit], after[2 * unit :]))
    hop_next, hop_prev = tensor_send(hop_next, 1, 0), tensor_send(hop_prev, 3, 1)
    same_slabs = assemble(*[(piece, 0, unit) for piece in (mine, before, after, hop_next)])
    other_slabs = assemble(
        *[(piece, 0, unit) for piece in (partner, before_other, after_other)],
        (hop_prev, unit, 2 * unit),
    )
    cots = assemble(
        (cotangent.reshape(2 * rows, columns), 0, 2 * rows),
        (before, 2 * unit, 4 * unit),
        (after, unit, 3 * unit),
        (hop_next, unit, 2 * unit),
        (hop_prev, 0, unit),
    )
    gathered, same_slabs, other_slabs, cots, weight = lax.optimization_barrier(
        (gathered, same_slabs, other_slabs, cots, key_value_weight)
    )

    def across(chip_step, core_flip):
        target = (chip + chip_step) % CHIPS * 2 + (core + core_flip) % 2
        start = target * window + (x + 2) % 4 * tile
        return lax.dynamic_slice_in_dim(weight, start, tile, 1).reshape(unit, columns)

    late = [
        jnp.concatenate([across(1, 0), across(2, 0)]),
        jnp.concatenate([across(3, 0), across(2, 1)]),
        *[across(*step) for step in ((1, 1), (3, 1), (0, 1), (0, 0))],
    ]

    low, weighted_value, coef = call(
        low_kernel,
        [SMEM] * 4 + [VMEM] * 3,
        [shape((rows, 2 * RANK), F32), shape((rows, columns), BF), shape((rows, 1), F32)],
        2 * rows * RANK * window,
        16,
    )(
        slots,
        live_rows_of_block,
        prompt_of_block,
        reward_of_block,
        gathered,
        normed_input_rows,
        cotangent,
    )
    low = (low + tensor_send(low, 0, 1)).astype(BF)
    lows = [low] + [tensor_send(low, s, 0) for s in (1, 3, 2)]
    same_left, same_right = x_send(same_slabs, 1), x_send(same_slabs, 3)

    terms, low = call(
        terms_kernel,
        [SMEM] + [VMEM] * 6,
        [shape((dp, owned, window + columns), BF), shape((rows, 2 * RANK), BF)],
        4 * rows * RANK * window,
        16,
    )(slots, *lows, normed_input_rows, weighted_value)
    cots_other = tensor_send(cots, 0, 1)
    terms, same_left, same_right, other_slabs, cots, cots_other, late = lax.optimization_barrier(
        (terms, same_left, same_right, other_slabs, cots, cots_other, late)
    )
    other_left, other_right = x_send(other_slabs, 1), x_send(other_slabs, 3)
    terms = lax.all_to_all(terms, "dp", 0, 0)
    routes = (1, 0), (3, 0), (1, 1), (3, 1), (0, 1)
    before, after, before_other, after_other, partner = [
        tensor_send(v, *route) for v, route in zip(late[:5], routes, strict=True)
    ]
    hop_next, hop_prev = lax.optimization_barrier((before[unit:], after[unit:]))
    slabs_far = [
        late[5], before, after, tensor_send(hop_next, 1, 0),
        partner, before_other, after_other, tensor_send(hop_prev, 3, 1),
    ]
    quarters = (x + jnp.array([0, 3, 1, 2], jnp.int32)) % 4
    input_gradient = frozen_and_correction(
        slots,
        quarters,
        (cots, cots_other),
        (gathered, low, coef),
        (same_slabs, other_slabs, same_left, other_left, same_right, other_right),
        slabs_far,
        window,
    )
    grad_a, grad_b = call(
        sum_kernel,
        [VMEM],
        [shape((owned, window), F32), shape((owned, columns), F32)],
        0,
        8,
    )(terms)
    return (input_gradient, grad_a, grad_b)


def solution(mesh):
    in_specs = (
        P("dp", "tensor"),
        P("dp", None, "tensor"),
        P(None, None, "tensor"),
        P("dp", "tensor"),
        P("dp", "tensor"),
        P(),
        P("dp"),
        P("dp"),
        P("dp"),
        P("dp"),
    )
    out_specs = (P("dp", "tensor"), P("dp", "tensor"), P("dp", "tensor"))
    return jax.shard_map(shards, mesh=mesh, in_specs=in_specs, out_specs=out_specs, check_vma=False)
```

```python
import functools

import jax
import jax.numpy as jnp
from jax import lax
from jax.experimental import pallas as pl
from jax.experimental.pallas import tpu as pltpu
from jax.sharding import PartitionSpec as P

BLOCK = 128
GSIZE = 8
SLOTS = 8
RANK = 64
LANES = 128
CHIPS = 4
FULL_VMEM = 60 * 2**20
LOWRANK_MULTIPLIER = 2.0
BF = jnp.bfloat16
F32 = jnp.float32
VMEM = pl.BlockSpec(memory_space=pltpu.VMEM)
SMEM = pl.BlockSpec(memory_space=pltpu.SMEM)


def dot(a, b, ca, cb):
    return lax.dot_general(a, b, (((ca,), (cb,)), ((), ())), preferred_element_type=F32)


def call(kernel, in_specs, shapes, flops, mib):
    single = not isinstance(shapes, (list, tuple))
    shapes = [shapes] if single else list(shapes)
    return pl.pallas_call(
        kernel,
        in_specs=in_specs,
        out_specs=VMEM if single else [VMEM] * len(shapes),
        out_shape=shapes[0] if single else shapes,
        compiler_params=pltpu.CompilerParams(vmem_limit_bytes=mib * 2**20),
        cost_estimate=pl.CostEstimate(flops=flops, bytes_accessed=2**20, transcendentals=0),
    )


def tensor_send(value, chip_step, core_flip):
    pairs = [
        (y * 2 + c, (y + chip_step) % CHIPS * 2 + (c ^ core_flip))
        for y in range(CHIPS)
        for c in range(2)
    ]
    return lax.ppermute(value, "tensor", pairs)


def x_send(value, step):
    pairs = [(i, i // 4 * 4 + (i + step) % 4) for i in range(lax.axis_size("dp"))]
    return lax.ppermute(value, "dp", pairs)


def pack_kernel(prompt, reward, down_ref, up_ref, out_ref):
    shape = (down_ref.shape[0], LANES)
    row = lax.broadcasted_iota(jnp.int32, shape, 0)
    lane = lax.broadcasted_iota(jnp.int32, shape, 1)
    blocks = reward.shape[1]
    rewards = jnp.zeros(shape, F32)
    prompts = jnp.full(shape, -1.0, F32)
    for b in range(blocks):
        one = (slice(0, 1), slice(b, b + 1))
        rewards = jnp.where(lane % blocks == b, reward[one], rewards)
        prompts = jnp.where(lane == b, prompt[one].astype(F32), prompts)
    high = rewards.astype(BF).astype(F32)
    rest = rewards - high
    middle = rest.astype(BF).astype(F32)
    part = lane // blocks
    parts = jnp.where(part == 0, high, jnp.where(part == 1, middle, rest - middle))
    parts = jnp.where(part < 3, parts, 0.0)
    facts = jnp.where(row == 0, parts, jnp.where(row == 1, prompts, 0.0)).astype(BF)
    packed = jnp.concatenate([down_ref[...], up_ref[...], facts], axis=1)
    for i in range(out_ref.shape[0]):
        out_ref[i] = packed


def streamed(kernel, blocks, out):
    whole = lambda shape: pl.BlockSpec(shape, lambda i: (0,) * len(shape))
    return pl.pallas_call(
        kernel,
        grid=(1,),
        in_specs=[whole(shape) for shape in blocks],
        out_specs=whole(out),
        out_shape=jax.ShapeDtypeStruct(out, BF),
        compiler_params=pltpu.CompilerParams(vmem_limit_bytes=FULL_VMEM),
    )


def assemble_kernel(cuts, *refs):
    *pieces, out_ref, done = refs
    copies = []
    at = 0
    for i, (piece, (start, stop)) in enumerate(zip(pieces, cuts, strict=True)):
        size = stop - start
        source, target = piece.at[pl.ds(start, size)], out_ref.at[pl.ds(at, size)]
        copies.append(pltpu.make_async_copy(source, target, done.at[i]))
        at += size
    for copy in copies:
        copy.start()
    for copy in copies:
        copy.wait()


def assemble(*pieces):
    arrays = [p[0] for p in pieces]
    cuts = [p[1:] for p in pieces]
    columns = arrays[0].shape[1]
    total = sum(stop - start for start, stop in cuts)
    return pl.pallas_call(
        functools.partial(assemble_kernel, cuts),
        in_specs=[pl.BlockSpec(memory_space=pl.ANY)] * len(arrays),
        out_specs=pl.BlockSpec(memory_space=pltpu.HBM),
        out_shape=jax.ShapeDtypeStruct((total, columns), BF),
        scratch_shapes=[pltpu.SemaphoreType.DMA((len(arrays),))],
        compiler_params=pltpu.CompilerParams(vmem_limit_bytes=4 * 2**20),
    )(*arrays)


def payload_kernel(places, *refs):
    *slabs, cot_ref, next_ref, next_other, prev_ref, prev_other, mine_ref, other_ref = refs
    tile, rows = slabs[0].shape[1], cot_ref.shape[1]
    key, value = (cot_ref.at[0],), (cot_ref.at[1],)
    slab = lambda i: (slabs[i].at[0], slabs[i].at[1])
    orders = (
        (next_ref, (slab(0), slab(2), key, value)),
        (next_other, (slab(1),)),
        (prev_ref, (slab(3), key, value, slab(5))),
        (prev_other, (slab(4),)),
        (mine_ref, (slab(6),)),
        (other_ref, (slab(7),)),
    )
    for out_ref, units in orders:
        at = 0
        for piece in (p for unit in units for p in unit):
            out_ref[at : at + piece.shape[0]] = piece[...]
            at += piece.shape[0]


def payloads(places, weight, cotangent, tile):
    columns = weight.shape[2]
    slab = [
        pl.BlockSpec((2, tile, columns), lambda g, p, i=i: (0, p[i], 0)) for i in range(8)
    ]
    sizes = [n * 2 * tile for n in (4, 1, 4, 1, 1, 1)]
    return pl.pallas_call(
        payload_kernel,
        grid_spec=pltpu.PrefetchScalarGridSpec(
            num_scalar_prefetch=1,
            grid=(1,),
            in_specs=[*slab, pl.BlockSpec(cotangent.shape, lambda g, p: (0, 0, 0))],
            out_specs=[pl.BlockSpec((n, columns), lambda g, p: (0, 0)) for n in sizes],
        ),
        out_shape=[jax.ShapeDtypeStruct((n, columns), BF) for n in sizes],
        compiler_params=pltpu.CompilerParams(vmem_limit_bytes=FULL_VMEM),
    )(places, *[weight] * 8, cotangent)


def factor_rows(ref, slot, start, size):
    owners = ref.shape[0] // SLOTS
    return ref[pl.ds(slot * owners, owners), :, pl.ds(start, size)].reshape(RANK, size)


def low_kernel(
    slots, live, prompt, reward, gathered_ref, x_ref, cot_ref, low_ref, weighted_ref, coef_ref
):
    window = x_ref.shape[1]
    columns = cot_ref.shape[2]
    blocks = reward.shape[0]
    facts = gathered_ref[:, :, window + columns :].astype(F32)
    row = lax.broadcasted_iota(jnp.int32, facts.shape, 1)
    parts = jnp.sum(jnp.where(row == 0, facts, 0.0), axis=1)
    prompts = jnp.sum(jnp.where(row == 1, facts, 0.0), axis=1)
    rewards = parts + pltpu.roll(parts, LANES - blocks, 1)
    rewards = rewards + pltpu.roll(parts, LANES - 2 * blocks, 1)
    place = lax.broadcasted_iota(jnp.int32, (BLOCK, 1), 0)
    whole = lambda v: jnp.sum(jnp.sum(v, axis=1, keepdims=True), axis=0, keepdims=True)
    for b in range(blocks):
        same = prompts == prompt[b].astype(F32)
        mean = whole(jnp.where(same, rewards, 0.0)) / GSIZE
        square = whole(jnp.where(same, rewards * rewards, 0.0)) / GSIZE
        spread = jnp.sqrt(jnp.maximum(square - mean * mean, 1.0))
        advantage = (reward[b] - mean) / spread
        coef = jnp.where(place < live[b], -advantage / GSIZE, 0.0)
        rows = pl.ds(b * BLOCK, BLOCK)
        weighted = (cot_ref[1, rows, :].astype(F32) * coef).astype(BF)
        low_h = dot(x_ref[rows, :], factor_rows(gathered_ref, slots[b], 0, window), 1, 1)
        low_g = dot(weighted, factor_rows(gathered_ref, slots[b], window, columns), 1, 1)
        low_ref[rows, :] = jnp.concatenate([low_h, low_g], axis=1)
        weighted_ref[rows, :] = weighted
        coef_ref[rows, :] = coef


def terms_kernel(slots, own, first, second, third, x_ref, weighted_ref, terms_ref, low_ref):
    window = x_ref.shape[1]
    columns = weighted_ref.shape[1]
    owners, owned = terms_ref.shape[0] // SLOTS, terms_ref.shape[1]
    low = own[...].astype(F32) + first[...].astype(F32)
    low = (low + second[...].astype(F32)) + third[...].astype(F32)
    low_ref[...] = low.astype(BF)
    for i in range(terms_ref.shape[0]):
        terms_ref[i] = jnp.zeros(terms_ref.shape[1:], BF)
    for b in range(x_ref.shape[0] // BLOCK):
        rows = pl.ds(b * BLOCK, BLOCK)
        low = low_ref[rows, :]
        down = LOWRANK_MULTIPLIER * dot(low, x_ref[rows, :], 0, 0)[RANK:]
        up = LOWRANK_MULTIPLIER * dot(low, weighted_ref[rows, :], 0, 0)[:RANK]
        place = pl.ds(slots[b] * owners, owners)
        terms_ref[place, :, :window] = down.astype(BF).reshape(owners, owned, window)
        terms_ref[place, :, window:] = up.astype(BF).reshape(owners, owned, columns)


def quarter(weighted, parts, low_ref, gathered_ref, slots, start, tile):
    slabs = [p[i * tile : (i + 1) * tile] for p in parts for i in range(p.shape[0] // tile)]
    total = dot(weighted[...], jnp.concatenate(slabs, axis=1), 1, 1)
    extra = []
    for b in range(total.shape[0] // BLOCK):
        factor = factor_rows(gathered_ref, slots[b], start, tile)
        factor = jnp.concatenate([jnp.zeros_like(factor), factor], axis=0)
        low = low_ref[b * BLOCK : (b + 1) * BLOCK, :]
        extra.append(LOWRANK_MULTIPLIER * dot(low, factor, 1, 0))
    return (total + jnp.concatenate(extra, axis=0)).astype(BF)


def near_kernel(slots, quarters, cots, others, gathered_ref, low_ref, coef_ref, *refs):
    *slabs, out_ref, weighted = refs
    rows, columns = coef_ref.shape[0], cots.shape[1]
    tile = rows // 2
    coef = coef_ref[...]
    count = cots.shape[0] // rows
    for i in range(2 * count):
        source = (cots, others)[(i // count + (i % count == count - 1)) % 2]
        piece = source[i % count * rows : (i % count + 1) * rows]
        weighted[:, i * columns : (i + 1) * columns] = (piece.astype(F32) * coef).astype(BF)
    for r, part in enumerate(slabs):
        start = pl.multiple_of(quarters[r] * tile, tile)
        out_ref[:, pl.ds(start, tile)] = quarter(
            weighted, (part,), low_ref, gathered_ref, slots, start, tile
        )


def far_kernel(slots, quarters, near_ref, weighted, gathered_ref, low_ref, *refs):
    *parts, out_ref = refs
    tile = out_ref.shape[1]
    parts = [ref.at[pl.ds(0, 2 * tile)] for ref in parts]
    out_ref[...] = quarter(weighted, parts, low_ref, gathered_ref, slots, 0, tile)


def frozen_and_correction(slots, quarters, cots, adapter, near, far, window):
    gathered, low, coef = adapter
    rows, columns, tile = coef.shape[0], cots[0].shape[1], window // 4
    depth = 2 * cots[0].shape[0] // rows * columns
    shape = jax.ShapeDtypeStruct
    whole = lambda dims: pl.BlockSpec(dims, lambda i, *_: (0,) * len(dims))
    streams = [*cots, gathered, low, coef, *near]
    partial, weighted = pl.pallas_call(
        near_kernel,
        grid_spec=pltpu.PrefetchScalarGridSpec(
            num_scalar_prefetch=2,
            grid=(1,),
            in_specs=[whole(v.shape) for v in streams],
            out_specs=[whole((rows, window)), whole((rows, depth))],
        ),
        out_shape=[shape((rows, window), BF), shape((rows, depth), BF)],
        compiler_params=pltpu.CompilerParams(vmem_limit_bytes=FULL_VMEM // 2),
    )(slots, quarters, *streams)
    owners, owned = gathered.shape[:2]
    return pl.pallas_call(
        far_kernel,
        grid_spec=pltpu.PrefetchScalarGridSpec(
            num_scalar_prefetch=2,
            grid=(1,),
            in_specs=[
                pl.BlockSpec(memory_space=pl.ANY),
                whole(weighted.shape),
                pl.BlockSpec((owners, owned, tile), lambda i, s, q: (0, 0, q[3])),
                whole(low.shape),
                *[whole(v.shape) for v in far],
            ],
            out_specs=pl.BlockSpec((rows, tile), lambda i, s, q: (0, q[3])),
        ),
        out_shape=shape((rows, window), BF),
        input_output_aliases={2: 0},
        compiler_params=pltpu.CompilerParams(vmem_limit_bytes=FULL_VMEM // 2),
    )(slots, quarters, partial, weighted, gathered, low, *far)


def sum_kernel(terms_ref, down_ref, up_ref):
    window = down_ref.shape[1]
    total = terms_ref[0].astype(F32)
    for i in range(1, terms_ref.shape[0]):
        total = total + terms_ref[i].astype(F32)
    down_ref[...] = total[:, :window]
    up_ref[...] = total[:, window:]


def shards(
    normed_input_rows,
    key_value_cotangent,
    key_value_weight,
    adapter_down_factors,
    adapter_up_factors,
    slot_adapter,
    adapter_of_block,
    live_rows_of_block,
    prompt_of_block,
    reward_of_block,
):
    rows, window = normed_input_rows.shape
    columns = key_value_cotangent.shape[2]
    dp = lax.axis_size("dp")
    owned = adapter_down_factors.shape[0]
    te = lax.axis_index("tensor")
    chip, core = te // 2, te % 2
    x = lax.axis_index("dp") % 4
    tile = window // 4
    shape = jax.ShapeDtypeStruct
    slots = jnp.sum(
        jnp.where(
            adapter_of_block[:, None] == slot_adapter[None, :], jnp.arange(SLOTS, dtype=jnp.int32), 0
        ),
        axis=1,
    )

    packed = streamed(
        pack_kernel,
        [(1, 4), (1, 4), (owned, window), (owned, columns)],
        (dp, owned, window + columns + LANES),
    )(
        prompt_of_block.reshape(1, -1),
        reward_of_block.reshape(1, -1),
        adapter_down_factors,
        adapter_up_factors,
    )
    gathered = lax.all_to_all(packed, "dp", 0, 0)

    cotangent = jnp.transpose(key_value_cotangent, (1, 0, 2))
    steps = jnp.array([[1, 0], [1, 1], [2, 0], [3, 0], [3, 1], [2, 1], [0, 0], [0, 1]], jnp.int32)
    targets = (chip + steps[:, 0]) % CHIPS * 2 + (core + steps[:, 1]) % 2
    to_next, next_other, to_prev, prev_other, mine, other = payloads(
        targets * 4 + x, key_value_weight, cotangent, tile
    )
    before, after = tensor_send(to_next, 1, 0), tensor_send(to_prev, 3, 0)
    before_other, after_other = tensor_send(next_other, 1, 1), tensor_send(prev_other, 3, 1)
    partner = tensor_send(other, 0, 1)
    unit = 2 * tile
    hop_next, hop_prev = lax.optimization_barrier((before[unit : 3 * unit], after[2 * unit :]))
    hop_next, hop_prev = tensor_send(hop_next, 1, 0), tensor_send(hop_prev, 3, 1)
    slabs = assemble(
        *[(piece, 0, unit) for piece in (mine, before, after, hop_next)],
        *[(piece, 0, unit) for piece in (partner, before_other, after_other)],
        (hop_prev, unit, 2 * unit),
    )
    cots = assemble(
        (cotangent.reshape(2 * rows, columns), 0, 2 * rows),
        (before, 2 * unit, 4 * unit),
        (after, unit, 3 * unit),
        (hop_next, unit, 2 * unit),
        (hop_prev, 0, unit),
    )
    gathered, slabs, cots, weight = lax.optimization_barrier(
        (gathered, slabs, cots, key_value_weight)
    )

    def across(chip_step, core_flip):
        target = (chip + chip_step) % CHIPS * 2 + (core + core_flip) % 2
        start = target * window + (x + 2) % 4 * tile
        return lax.dynamic_slice_in_dim(weight, start, tile, 1).reshape(unit, columns)

    late = [
        jnp.concatenate([across(1, 0), across(2, 0)]),
        jnp.concatenate([across(3, 0), across(2, 1)]),
        *[across(*step) for step in ((1, 1), (3, 1), (0, 1), (0, 0))],
    ]

    low, weighted_value, coef = call(
        low_kernel,
        [SMEM] * 4 + [VMEM] * 3,
        [shape((rows, 2 * RANK), F32), shape((rows, columns), BF), shape((rows, 1), F32)],
        2 * rows * RANK * window,
        16,
    )(
        slots,
        live_rows_of_block,
        prompt_of_block,
        reward_of_block,
        gathered,
        normed_input_rows,
        cotangent,
    )
    low = (low + tensor_send(low, 0, 1)).astype(BF)
    lows = [low] + [tensor_send(low, s, 0) for s in (1, 3, 2)]
    slabs_left, slabs_right = x_send(slabs, 1), x_send(slabs, 3)

    terms, low = call(
        terms_kernel,
        [SMEM] + [VMEM] * 6,
        [shape((dp, owned, window + columns), BF), shape((rows, 2 * RANK), BF)],
        4 * rows * RANK * window,
        16,
    )(slots, *lows, normed_input_rows, weighted_value)
    cots_other = tensor_send(cots, 0, 1)
    terms, slabs_left, slabs_right, cots, cots_other, late = lax.optimization_barrier(
        (terms, slabs_left, slabs_right, cots, cots_other, late)
    )
    terms = lax.all_to_all(terms, "dp", 0, 0)
    routes = (1, 0), (3, 0), (1, 1), (3, 1), (0, 1)
    before, after, before_other, after_other, partner = [
        tensor_send(v, *route) for v, route in zip(late[:5], routes, strict=True)
    ]
    hop_next, hop_prev = lax.optimization_barrier((before[unit:], after[unit:]))
    slabs_far = [
        late[5], before, after, tensor_send(hop_next, 1, 0),
        partner, before_other, after_other, tensor_send(hop_prev, 3, 1),
    ]
    quarters = (x + jnp.array([0, 3, 1, 2], jnp.int32)) % 4
    input_gradient = frozen_and_correction(
        slots,
        quarters,
        (cots, cots_other),
        (gathered, low, coef),
        (slabs, slabs_left, slabs_right),
        slabs_far,
        window,
    )
    grad_a, grad_b = call(
        sum_kernel,
        [VMEM],
        [shape((owned, window), F32), shape((owned, columns), F32)],
        0,
        8,
    )(terms)
    return (input_gradient, grad_a, grad_b)


def solution(mesh):
    in_specs = (
        P("dp", "tensor"),
        P("dp", None, "tensor"),
        P(None, None, "tensor"),
        P("dp", "tensor"),
        P("dp", "tensor"),
        P(),
        P("dp"),
        P("dp"),
        P("dp"),
        P("dp"),
    )
    out_specs = (P("dp", "tensor"), P("dp", "tensor"), P("dp", "tensor"))
    return jax.shard_map(shards, mesh=mesh, in_specs=in_specs, out_specs=out_specs, check_vma=False)
```

```python
import functools

import jax
import jax.numpy as jnp
from jax import lax
from jax.experimental import pallas as pl
from jax.experimental.pallas import tpu as pltpu
from jax.sharding import PartitionSpec as P

BLOCK = 128
GSIZE = 8
SLOTS = 8
RANK = 64
LANES = 128
CHIPS = 4
FULL_VMEM = 60 * 2**20
LOWRANK_MULTIPLIER = 2.0
BF = jnp.bfloat16
F32 = jnp.float32
VMEM = pl.BlockSpec(memory_space=pltpu.VMEM)
SMEM = pl.BlockSpec(memory_space=pltpu.SMEM)


def dot(a, b, ca, cb):
    return lax.dot_general(a, b, (((ca,), (cb,)), ((), ())), preferred_element_type=F32)


def call(kernel, in_specs, shapes, flops, mib):
    single = not isinstance(shapes, (list, tuple))
    shapes = [shapes] if single else list(shapes)
    return pl.pallas_call(
        kernel,
        in_specs=in_specs,
        out_specs=VMEM if single else [VMEM] * len(shapes),
        out_shape=shapes[0] if single else shapes,
        compiler_params=pltpu.CompilerParams(vmem_limit_bytes=mib * 2**20),
        cost_estimate=pl.CostEstimate(flops=flops, bytes_accessed=2**20, transcendentals=0),
    )


def tensor_send(value, chip_step, core_flip):
    pairs = [
        (y * 2 + c, (y + chip_step) % CHIPS * 2 + (c ^ core_flip))
        for y in range(CHIPS)
        for c in range(2)
    ]
    return lax.ppermute(value, "tensor", pairs)


def x_send(value, step):
    pairs = [(i, i // 4 * 4 + (i + step) % 4) for i in range(lax.axis_size("dp"))]
    return lax.ppermute(value, "dp", pairs)


def pack_kernel(prompt, reward, down_ref, up_ref, out_ref):
    shape = (down_ref.shape[0], LANES)
    row = lax.broadcasted_iota(jnp.int32, shape, 0)
    lane = lax.broadcasted_iota(jnp.int32, shape, 1)
    blocks = reward.shape[1]
    rewards = jnp.zeros(shape, F32)
    prompts = jnp.full(shape, -1.0, F32)
    for b in range(blocks):
        one = (slice(0, 1), slice(b, b + 1))
        rewards = jnp.where(lane % blocks == b, reward[one], rewards)
        prompts = jnp.where(lane == b, prompt[one].astype(F32), prompts)
    high = rewards.astype(BF).astype(F32)
    rest = rewards - high
    middle = rest.astype(BF).astype(F32)
    part = lane // blocks
    parts = jnp.where(part == 0, high, jnp.where(part == 1, middle, rest - middle))
    parts = jnp.where(part < 3, parts, 0.0)
    facts = jnp.where(row == 0, parts, jnp.where(row == 1, prompts, 0.0)).astype(BF)
    packed = jnp.concatenate([down_ref[...], up_ref[...], facts], axis=1)
    for i in range(out_ref.shape[0]):
        out_ref[i] = packed


def streamed(kernel, blocks, out):
    whole = lambda shape: pl.BlockSpec(shape, lambda i: (0,) * len(shape))
    return pl.pallas_call(
        kernel,
        grid=(1,),
        in_specs=[whole(shape) for shape in blocks],
        out_specs=whole(out),
        out_shape=jax.ShapeDtypeStruct(out, BF),
        compiler_params=pltpu.CompilerParams(vmem_limit_bytes=FULL_VMEM),
    )


def assemble_kernel(cuts, *refs):
    *pieces, out_ref = refs
    at = 0
    for piece, (start, stop) in zip(pieces, cuts, strict=True):
        out_ref[at : at + stop - start] = piece[start:stop]
        at += stop - start


def assemble(*pieces):
    arrays = [p[0] for p in pieces]
    cuts = [p[1:] for p in pieces]
    columns = arrays[0].shape[1]
    total = sum(stop - start for start, stop in cuts)
    whole = lambda shape: pl.BlockSpec(shape, lambda i: (0,) * len(shape))
    return pl.pallas_call(
        functools.partial(assemble_kernel, cuts),
        grid=(1,),
        in_specs=[whole(v.shape) for v in arrays],
        out_specs=whole((total, columns)),
        out_shape=jax.ShapeDtypeStruct((total, columns), BF),
        compiler_params=pltpu.CompilerParams(vmem_limit_bytes=FULL_VMEM),
    )(*arrays)


def payload_kernel(places, *refs):
    *slabs, cot_ref, next_ref, next_other, prev_ref, prev_other, mine_ref, other_ref = refs
    tile, rows = slabs[0].shape[1], cot_ref.shape[1]
    key, value = (cot_ref.at[0],), (cot_ref.at[1],)
    slab = lambda i: (slabs[i].at[0], slabs[i].at[1])
    orders = (
        (next_ref, (slab(0), slab(2), key, value)),
        (next_other, (slab(1),)),
        (prev_ref, (slab(3), key, value, slab(5))),
        (prev_other, (slab(4),)),
        (mine_ref, (slab(6),)),
        (other_ref, (slab(7),)),
    )
    for out_ref, units in orders:
        at = 0
        for piece in (p for unit in units for p in unit):
            out_ref[at : at + piece.shape[0]] = piece[...]
            at += piece.shape[0]


def payloads(places, weight, cotangent, tile):
    columns = weight.shape[2]
    slab = [
        pl.BlockSpec((2, tile, columns), lambda g, p, i=i: (0, p[i], 0)) for i in range(8)
    ]
    sizes = [n * 2 * tile for n in (4, 1, 4, 1, 1, 1)]
    return pl.pallas_call(
        payload_kernel,
        grid_spec=pltpu.PrefetchScalarGridSpec(
            num_scalar_prefetch=1,
            grid=(1,),
            in_specs=[*slab, pl.BlockSpec(cotangent.shape, lambda g, p: (0, 0, 0))],
            out_specs=[pl.BlockSpec((n, columns), lambda g, p: (0, 0)) for n in sizes],
        ),
        out_shape=[jax.ShapeDtypeStruct((n, columns), BF) for n in sizes],
        compiler_params=pltpu.CompilerParams(vmem_limit_bytes=FULL_VMEM),
    )(places, *[weight] * 8, cotangent)


def factor_rows(ref, slot, start, size):
    owners = ref.shape[0] // SLOTS
    return ref[pl.ds(slot * owners, owners), :, pl.ds(start, size)].reshape(RANK, size)


def low_kernel(
    slots, live, prompt, reward, gathered_ref, x_ref, cot_ref, low_ref, weighted_ref, coef_ref
):
    window = x_ref.shape[1]
    columns = cot_ref.shape[2]
    blocks = reward.shape[0]
    facts = gathered_ref[:, :, window + columns :].astype(F32)
    row = lax.broadcasted_iota(jnp.int32, facts.shape, 1)
    parts = jnp.sum(jnp.where(row == 0, facts, 0.0), axis=1)
    prompts = jnp.sum(jnp.where(row == 1, facts, 0.0), axis=1)
    rewards = parts + pltpu.roll(parts, LANES - blocks, 1)
    rewards = rewards + pltpu.roll(parts, LANES - 2 * blocks, 1)
    place = lax.broadcasted_iota(jnp.int32, (BLOCK, 1), 0)
    whole = lambda v: jnp.sum(jnp.sum(v, axis=1, keepdims=True), axis=0, keepdims=True)
    for b in range(blocks):
        same = prompts == prompt[b].astype(F32)
        mean = whole(jnp.where(same, rewards, 0.0)) / GSIZE
        square = whole(jnp.where(same, rewards * rewards, 0.0)) / GSIZE
        spread = jnp.sqrt(jnp.maximum(square - mean * mean, 1.0))
        advantage = (reward[b] - mean) / spread
        coef = jnp.where(place < live[b], -advantage / GSIZE, 0.0)
        rows = pl.ds(b * BLOCK, BLOCK)
        weighted = (cot_ref[1, rows, :].astype(F32) * coef).astype(BF)
        low_h = dot(x_ref[rows, :], factor_rows(gathered_ref, slots[b], 0, window), 1, 1)
        low_g = dot(weighted, factor_rows(gathered_ref, slots[b], window, columns), 1, 1)
        low_ref[rows, :] = jnp.concatenate([low_h, low_g], axis=1)
        weighted_ref[rows, :] = weighted
        coef_ref[rows, :] = coef


def terms_kernel(slots, own, first, second, third, x_ref, weighted_ref, terms_ref, low_ref):
    window = x_ref.shape[1]
    columns = weighted_ref.shape[1]
    owners, owned = terms_ref.shape[0] // SLOTS, terms_ref.shape[1]
    low = own[...].astype(F32) + first[...].astype(F32)
    low = (low + second[...].astype(F32)) + third[...].astype(F32)
    low_ref[...] = low.astype(BF)
    for i in range(terms_ref.shape[0]):
        terms_ref[i] = jnp.zeros(terms_ref.shape[1:], BF)
    for b in range(x_ref.shape[0] // BLOCK):
        rows = pl.ds(b * BLOCK, BLOCK)
        low = low_ref[rows, :]
        down = LOWRANK_MULTIPLIER * dot(low, x_ref[rows, :], 0, 0)[RANK:]
        up = LOWRANK_MULTIPLIER * dot(low, weighted_ref[rows, :], 0, 0)[:RANK]
        place = pl.ds(slots[b] * owners, owners)
        terms_ref[place, :, :window] = down.astype(BF).reshape(owners, owned, window)
        terms_ref[place, :, window:] = up.astype(BF).reshape(owners, owned, columns)


def quarter(weighted, parts, low_ref, gathered_ref, slots, start, tile):
    slabs = [p[i * tile : (i + 1) * tile] for p in parts for i in range(p.shape[0] // tile)]
    total = dot(weighted[...], jnp.concatenate(slabs, axis=1), 1, 1)
    extra = []
    for b in range(total.shape[0] // BLOCK):
        factor = factor_rows(gathered_ref, slots[b], start, tile)
        factor = jnp.concatenate([jnp.zeros_like(factor), factor], axis=0)
        low = low_ref[b * BLOCK : (b + 1) * BLOCK, :]
        extra.append(LOWRANK_MULTIPLIER * dot(low, factor, 1, 0))
    return (total + jnp.concatenate(extra, axis=0)).astype(BF)


def near_kernel(slots, quarters, cots, others, gathered_ref, low_ref, coef_ref, *refs):
    *slabs, out_ref, weighted = refs
    rows, columns = coef_ref.shape[0], cots.shape[1]
    tile = rows // 2
    coef = coef_ref[...]
    count = cots.shape[0] // rows
    for i in range(2 * count):
        source = (cots, others)[(i // count + (i % count == count - 1)) % 2]
        piece = source[i % count * rows : (i % count + 1) * rows]
        weighted[:, i * columns : (i + 1) * columns] = (piece.astype(F32) * coef).astype(BF)
    for r, part in enumerate(slabs):
        start = pl.multiple_of(quarters[r] * tile, tile)
        out_ref[:, pl.ds(start, tile)] = quarter(
            weighted, (part,), low_ref, gathered_ref, slots, start, tile
        )


def far_kernel(slots, quarters, near_ref, weighted, gathered_ref, low_ref, *refs):
    *parts, out_ref = refs
    tile = out_ref.shape[1]
    parts = [ref.at[pl.ds(0, 2 * tile)] for ref in parts]
    out_ref[...] = quarter(weighted, parts, low_ref, gathered_ref, slots, 0, tile)


def frozen_and_correction(slots, quarters, cots, adapter, near, far, window):
    gathered, low, coef = adapter
    rows, columns, tile = coef.shape[0], cots[0].shape[1], window // 4
    depth = 2 * cots[0].shape[0] // rows * columns
    shape = jax.ShapeDtypeStruct
    whole = lambda dims: pl.BlockSpec(dims, lambda i, *_: (0,) * len(dims))
    streams = [*cots, gathered, low, coef, *near]
    partial, weighted = pl.pallas_call(
        near_kernel,
        grid_spec=pltpu.PrefetchScalarGridSpec(
            num_scalar_prefetch=2,
            grid=(1,),
            in_specs=[whole(v.shape) for v in streams],
            out_specs=[whole((rows, window)), whole((rows, depth))],
        ),
        out_shape=[shape((rows, window), BF), shape((rows, depth), BF)],
        compiler_params=pltpu.CompilerParams(vmem_limit_bytes=FULL_VMEM // 2),
    )(slots, quarters, *streams)
    owners, owned = gathered.shape[:2]
    return pl.pallas_call(
        far_kernel,
        grid_spec=pltpu.PrefetchScalarGridSpec(
            num_scalar_prefetch=2,
            grid=(1,),
            in_specs=[
                pl.BlockSpec(memory_space=pl.ANY),
                whole(weighted.shape),
                pl.BlockSpec((owners, owned, tile), lambda i, s, q: (0, 0, q[3])),
                whole(low.shape),
                *[whole(v.shape) for v in far],
            ],
            out_specs=pl.BlockSpec((rows, tile), lambda i, s, q: (0, q[3])),
        ),
        out_shape=shape((rows, window), BF),
        input_output_aliases={2: 0},
        compiler_params=pltpu.CompilerParams(vmem_limit_bytes=FULL_VMEM // 2),
    )(slots, quarters, partial, weighted, gathered, low, *far)


def sum_kernel(terms_ref, down_ref, up_ref):
    window = down_ref.shape[1]
    total = terms_ref[0].astype(F32)
    for i in range(1, terms_ref.shape[0]):
        total = total + terms_ref[i].astype(F32)
    down_ref[...] = total[:, :window]
    up_ref[...] = total[:, window:]


def shards(
    normed_input_rows,
    key_value_cotangent,
    key_value_weight,
    adapter_down_factors,
    adapter_up_factors,
    slot_adapter,
    adapter_of_block,
    live_rows_of_block,
    prompt_of_block,
    reward_of_block,
):
    rows, window = normed_input_rows.shape
    columns = key_value_cotangent.shape[2]
    dp = lax.axis_size("dp")
    owned = adapter_down_factors.shape[0]
    te = lax.axis_index("tensor")
    chip, core = te // 2, te % 2
    x = lax.axis_index("dp") % 4
    tile = window // 4
    shape = jax.ShapeDtypeStruct
    slots = jnp.sum(
        jnp.where(
            adapter_of_block[:, None] == slot_adapter[None, :], jnp.arange(SLOTS, dtype=jnp.int32), 0
        ),
        axis=1,
    )

    packed = streamed(
        pack_kernel,
        [(1, 4), (1, 4), (owned, window), (owned, columns)],
        (dp, owned, window + columns + LANES),
    )(
        prompt_of_block.reshape(1, -1),
        reward_of_block.reshape(1, -1),
        adapter_down_factors,
        adapter_up_factors,
    )
    gathered = lax.all_to_all(packed, "dp", 0, 0)

    cotangent = jnp.transpose(key_value_cotangent, (1, 0, 2))
    steps = jnp.array([[1, 0], [1, 1], [2, 0], [3, 0], [3, 1], [2, 1], [0, 0], [0, 1]], jnp.int32)
    targets = (chip + steps[:, 0]) % CHIPS * 2 + (core + steps[:, 1]) % 2
    to_next, next_other, to_prev, prev_other, mine, other = payloads(
        targets * 4 + x, key_value_weight, cotangent, tile
    )
    before, after = tensor_send(to_next, 1, 0), tensor_send(to_prev, 3, 0)
    before_other, after_other = tensor_send(next_other, 1, 1), tensor_send(prev_other, 3, 1)
    partner = tensor_send(other, 0, 1)
    unit = 2 * tile
    hop_next, hop_prev = lax.optimization_barrier((before[unit : 3 * unit], after[2 * unit :]))
    hop_next, hop_prev = tensor_send(hop_next, 1, 0), tensor_send(hop_prev, 3, 1)
    slabs = assemble(
        *[(piece, 0, unit) for piece in (mine, before, after, hop_next)],
        *[(piece, 0, unit) for piece in (partner, before_other, after_other)],
        (hop_prev, unit, 2 * unit),
    )
    cots = assemble(
        (cotangent.reshape(2 * rows, columns), 0, 2 * rows),
        (before, 2 * unit, 4 * unit),
        (after, unit, 3 * unit),
        (hop_next, unit, 2 * unit),
        (hop_prev, 0, unit),
    )
    gathered, slabs, cots, weight = lax.optimization_barrier(
        (gathered, slabs, cots, key_value_weight)
    )

    def across(chip_step, core_flip):
        target = (chip + chip_step) % CHIPS * 2 + (core + core_flip) % 2
        start = target * window + (x + 2) % 4 * tile
        return lax.dynamic_slice_in_dim(weight, start, tile, 1).reshape(unit, columns)

    late = [
        jnp.concatenate([across(1, 0), across(2, 0)]),
        jnp.concatenate([across(3, 0), across(2, 1)]),
        *[across(*step) for step in ((1, 1), (3, 1), (0, 1), (0, 0))],
    ]

    low, weighted_value, coef = call(
        low_kernel,
        [SMEM] * 4 + [VMEM] * 3,
        [shape((rows, 2 * RANK), F32), shape((rows, columns), BF), shape((rows, 1), F32)],
        2 * rows * RANK * window,
        16,
    )(
        slots,
        live_rows_of_block,
        prompt_of_block,
        reward_of_block,
        gathered,
        normed_input_rows,
        cotangent,
    )
    low = (low + tensor_send(low, 0, 1)).astype(BF)
    lows = [low] + [tensor_send(low, s, 0) for s in (1, 3, 2)]
    slabs_left, slabs_right = x_send(slabs, 1), x_send(slabs, 3)

    terms, low = call(
        terms_kernel,
        [SMEM] + [VMEM] * 6,
        [shape((dp, owned, window + columns), BF), shape((rows, 2 * RANK), BF)],
        4 * rows * RANK * window,
        16,
    )(slots, *lows, normed_input_rows, weighted_value)
    cots_other = tensor_send(cots, 0, 1)
    terms, slabs_left, slabs_right, cots, cots_other, late = lax.optimization_barrier(
        (terms, slabs_left, slabs_right, cots, cots_other, late)
    )
    terms = lax.all_to_all(terms, "dp", 0, 0)
    routes = (1, 0), (3, 0), (1, 1), (3, 1), (0, 1)
    before, after, before_other, after_other, partner = [
        tensor_send(v, *route) for v, route in zip(late[:5], routes, strict=True)
    ]
    hop_next, hop_prev = lax.optimization_barrier((before[unit:], after[unit:]))
    slabs_far = [
        late[5], before, after, tensor_send(hop_next, 1, 0),
        partner, before_other, after_other, tensor_send(hop_prev, 3, 1),
    ]
    quarters = (x + jnp.array([0, 3, 1, 2], jnp.int32)) % 4
    input_gradient = frozen_and_correction(
        slots,
        quarters,
        (cots, cots_other),
        (gathered, low, coef),
        (slabs, slabs_left, slabs_right),
        slabs_far,
        window,
    )
    grad_a, grad_b = call(
        sum_kernel,
        [VMEM],
        [shape((owned, window), F32), shape((owned, columns), F32)],
        0,
        8,
    )(terms)
    return (input_gradient, grad_a, grad_b)


def solution(mesh):
    in_specs = (
        P("dp", "tensor"),
        P("dp", None, "tensor"),
        P(None, None, "tensor"),
        P("dp", "tensor"),
        P("dp", "tensor"),
        P(),
        P("dp"),
        P("dp"),
        P("dp"),
        P("dp"),
    )
    out_specs = (P("dp", "tensor"), P("dp", "tensor"), P("dp", "tensor"))
    return jax.shard_map(shards, mesh=mesh, in_specs=in_specs, out_specs=out_specs, check_vma=False)
```
